512 devices in a mesh: cols: 128 (over z, x, core), rep: 4 (over y).
Axes of the slice: x: 4, y: 4, z: 16, core: 2. Of those that a mesh axis runs over, the one named last changes fastest.
Arguments:
- features: bfloat16 [65536, 768], P(None, 'cols'), may hold values from -6 to 6
- self_ids: int32 [128, 32], P(None, 'rep'), may hold values from 0 to 65535
- nbr_ids: int32 [128, 32, 25], P(None, 'rep'), may hold values from 0 to 65535
- nbr_counts: int32 [128, 32], P(None, 'rep'), may hold values from 1 to 25
- w1_self: bfloat16 [768, 1024], P('cols'), may hold values from -0.21875 to 0.21875
- w1_nbr: bfloat16 [768, 1024], P('cols'), may hold values from -0.21875 to 0.21875
- bias1: float32 [1024], replicated, may hold values from -4 to 4
- w2_self: bfloat16 [1024, 153], replicated, may hold values from -0.25 to 0.25
- w2_nbr: bfloat16 [1024, 153], replicated, may hold values from -0.25 to 0.25
- bias2: float32 [153], replicated, may hold values from -4 to 4
- labels: int32 [4096], P(('cols', 'rep')), may hold values from 0 to 152, as said below
- top_ids: int32 [4096, 15], P(('cols', 'rep')), may hold values from 0 to 7
- top_counts: int32 [4096], P(('cols', 'rep')), may hold values from 1 to 15
Outputs:
- loss: float32 [], replicated
- grad_w1_self: float32 [768, 1024], P('cols')
- grad_w1_nbr: float32 [768, 1024], P('cols')
- grad_bias1: float32 [1024], replicated
- grad_w2_self: float32 [1024, 153], replicated
- grad_w2_nbr: float32 [1024, 153], replicated
- grad_bias2: float32 [153], replicated
The draws below stay inside these ranges and needn't reach their ends.
Inputs may be any that keep to these rules, and one draw needn't show every extreme that they name: `nbr_counts`: entries beyond a row's count are padding. `top_counts`: entries beyond a row's count are padding. `labels`: in each aligned block of 8 rows, the first 4 rows share one class; the others are drawn independently.
All inputs are finite; a program needn't handle non-finite values.
Results may differ from the reference program's by a relative error of at most 0.0037.
The reference program's roundings to bfloat16 on the way count: a program that leaves them out, or rounds other values in their place, can miss the bound.
Values may be sent and summed in bfloat16 or wider, within the bound.
A program may use at most 128 MiB of HBM per device.

```python
import jax
import jax.numpy as jnp
from jax import lax

F = 768
H = 1024
C = 153
FAN1 = 25
FAN2 = 15
ROWS_OWN = 8
NODES = 65536
OWNERS = 128
GROUP_ROWS = 32
TARGETS = 4096
N_COLS = 128
N_REP = 4


def draw_labels(key, part):
    key = jax.random.fold_in(key, 11)
    block_key = jax.random.fold_in(key, 1)
    row_key = jax.random.fold_in(key, 2)
    block_count = TARGETS // ROWS_OWN
    block_class = jax.random.randint(block_key, (block_count,), 0, C, dtype=jnp.int32)
    row_class = jax.random.randint(row_key, (TARGETS,), 0, C, dtype=jnp.int32)
    position = lax.broadcasted_iota(jnp.int32, (TARGETS,), 0)
    within = position % ROWS_OWN
    shared = jnp.repeat(block_class, ROWS_OWN)
    return jnp.where(within < max(ROWS_OWN // 2, 1), shared, row_class)


def with_ends(result, own_key, least, top_value):
    longest = result.shape.index(max(result.shape))
    spots = []
    for shift in (0, 1):
        where = [jax.random.randint(jax.random.fold_in(own_key, axis), (), 0, length) for axis, length in enumerate(result.shape)]
        where[longest] = (where[longest] + shift) % result.shape[longest]
        spots.append(tuple(where))
    return result.at[spots[0]].set(least).at[spots[1]].set(top_value)


def block_scale(own_key, extent, shards, least, high):
    level, own = 1.0, jax.random.fold_in(own_key, 6)
    for dim, blocks in shards:
        draws = jnp.exp(jax.random.uniform(jax.random.fold_in(own, dim), (blocks,), jnp.float32, least / len(shards), high / len(shards)))
        level = level * jnp.repeat(draws, extent[dim] // blocks).reshape([-1 if axis == dim else 1 for axis in range(len(extent))])
    return level


def centred(stream_key, extent, scale, most, pieces=(), held_as=jnp.bfloat16):
    entries = scale * jax.random.normal(stream_key, extent, jnp.float32)
    if pieces:
        entries = entries * block_scale(stream_key, extent, pieces, -0.22, 0.18)
    return jnp.clip(entries, -most, most).astype(held_as)


def setup_inputs(seed: int = 0) -> dict:
    streams_of = jax.random.split(jax.random.key(seed), 14)
    features = centred(streams_of[0], (NODES, F), 1.0, 6.0, ((1, 128),))
    self_ids = with_ends(jax.random.randint(streams_of[1], (OWNERS, GROUP_ROWS), 0, NODES), jax.random.fold_in(streams_of[1], 1), 0, NODES - 1).astype(jnp.int32)
    nbr_ids = with_ends(jax.random.randint(streams_of[2], (OWNERS, GROUP_ROWS, FAN1), 0, NODES), jax.random.fold_in(streams_of[2], 1), 0, NODES - 1).astype(jnp.int32)
    nbr_counts = with_ends(jax.random.randint(streams_of[3], (OWNERS, GROUP_ROWS), 1, FAN1 + 1), jax.random.fold_in(streams_of[3], 1), 1, FAN1).astype(jnp.int32)
    w1_self = centred(streams_of[4], (F, H), F ** -0.5, 0.21875, ((0, 128),))
    w1_nbr = centred(streams_of[5], (F, H), F ** -0.5, 0.21875, ((0, 128),))
    bias1 = centred(streams_of[6], (H,), 1.0, 4.0, (), jnp.float32)
    w2_self = centred(streams_of[7], (H, C), (H // 2) ** -0.5, 0.25)
    w2_nbr = centred(streams_of[8], (H, C), (H // 2) ** -0.5, 0.25)
    bias2 = centred(streams_of[9], (C,), 1.0, 4.0, (), jnp.float32)
    labels = draw_labels(jax.random.fold_in(streams_of[13], 71), 0)
    top_ids = with_ends(jax.random.randint(streams_of[11], (TARGETS, FAN2), 0, ROWS_OWN), jax.random.fold_in(streams_of[11], 1), 0, ROWS_OWN - 1).astype(jnp.int32)
    top_counts = with_ends(jax.random.randint(streams_of[12], (TARGETS,), 1, FAN2 + 1), jax.random.fold_in(streams_of[12], 1), 1, FAN2).astype(jnp.int32)
    return dict(features=features, self_ids=self_ids, nbr_ids=nbr_ids, nbr_counts=nbr_counts, w1_self=w1_self, w1_nbr=w1_nbr, bias1=bias1, w2_self=w2_self, w2_nbr=w2_nbr, bias2=bias2, labels=labels, top_ids=top_ids, top_counts=top_counts)


loss_scale = 64.0


def reference(features, self_ids, nbr_ids, nbr_counts, w1_self, w1_nbr, bias1, w2_self, w2_nbr, bias2, labels, top_ids, top_counts):
    targets = ROWS_OWN * N_COLS * N_REP
    blocks = targets // ROWS_OWN
    selfin = jnp.take(features, self_ids.reshape(targets), axis=0)
    id_blocks = nbr_ids.reshape(blocks, ROWS_OWN, FAN1)
    count_blocks = nbr_counts.reshape(blocks, ROWS_OWN)

    def block_mean(pair):
        node_ids, counts = pair
        picked = jnp.take(features, node_ids.reshape(ROWS_OWN * FAN1), axis=0).reshape(ROWS_OWN, FAN1, F).astype(jnp.float32)
        is_live = lax.broadcasted_iota(jnp.int32, (ROWS_OWN, FAN1), 1) < counts[:, None]
        summed = jnp.sum(jnp.where(is_live[:, :, None], picked, jnp.float32(0.0)), axis=1)
        return (summed / counts[:, None].astype(jnp.float32)).astype(jnp.bfloat16)

    nbrmean = lax.map(block_mean, (id_blocks, count_blocks)).reshape(targets, F)
    pre_act = jnp.dot(selfin, w1_self, preferred_element_type=jnp.float32) + jnp.dot(nbrmean, w1_nbr, preferred_element_type=jnp.float32) + bias1
    hidden = jnp.maximum(pre_act, 0.0).astype(jnp.bfloat16)
    top_live = lax.broadcasted_iota(jnp.int32, (targets, FAN2), 1) < top_counts[:, None]
    slots = lax.broadcasted_iota(jnp.int32, (1, 1, ROWS_OWN), 2)
    counts_matrix = jnp.sum(jnp.where(top_live[:, :, None] & (top_ids[:, :, None] == slots), jnp.float32(1.0), jnp.float32(0.0)), axis=1)
    counts_matrix = counts_matrix.reshape(blocks, ROWS_OWN, ROWS_OWN)
    top_div = top_counts.astype(jnp.float32)[:, None]
    hidden_blocks = hidden.reshape(blocks, ROWS_OWN, H).astype(jnp.float32)
    top_sum = jnp.einsum('brs,bsh->brh', counts_matrix, hidden_blocks, precision=lax.Precision.HIGHEST).reshape(targets, H)
    top_mean = (top_sum / top_div).astype(jnp.bfloat16)
    logits = jnp.dot(hidden, w2_self, preferred_element_type=jnp.float32) + jnp.dot(top_mean, w2_nbr, preferred_element_type=jnp.float32) + bias2
    exps = jnp.exp(logits)
    total = jnp.sum(exps, axis=1)
    onehot = jnp.where(lax.broadcasted_iota(jnp.int32, (targets, C), 1) == labels[:, None], jnp.float32(1.0), jnp.float32(0.0))
    row_loss = jnp.log(total) - jnp.sum(onehot * logits, axis=1)
    loss = jnp.sum(row_loss) / targets
    grad_logits = ((exps / total[:, None] - onehot) * (loss_scale / targets)).astype(jnp.bfloat16)
    grad_w2_self = jnp.dot(hidden.T, grad_logits, preferred_element_type=jnp.float32)
    grad_w2_nbr = jnp.dot(top_mean.T, grad_logits, preferred_element_type=jnp.float32)
    grad_bias2 = jnp.sum(grad_logits.astype(jnp.float32), axis=0)
    back_self = jnp.dot(grad_logits, w2_self.T, preferred_element_type=jnp.float32)
    back_top = jnp.dot(grad_logits, w2_nbr.T, preferred_element_type=jnp.float32) / top_div
    back_spread = jnp.einsum('brs,brh->bsh', counts_matrix, back_top.reshape(blocks, ROWS_OWN, H), precision=lax.Precision.HIGHEST).reshape(targets, H)
    back_hidden = back_self + back_spread
    grad_pre = jnp.where(pre_act > 0.0, back_hidden, jnp.float32(0.0)).astype(jnp.bfloat16)
    grad_w1_self = jnp.dot(selfin.T, grad_pre, preferred_element_type=jnp.float32)
    grad_w1_nbr = jnp.dot(nbrmean.T, grad_pre, preferred_element_type=jnp.float32)
    grad_bias1 = jnp.sum(grad_pre.astype(jnp.float32), axis=0)
    return (loss, grad_w1_self, grad_w1_nbr, grad_bias1, grad_w2_self, grad_w2_nbr, grad_bias2)
```

```python
import jax
import jax.numpy as jnp
from jax import lax
from jax.experimental import pallas as pl
from jax.experimental.pallas import tpu as pltpu
from jax.sharding import PartitionSpec as P

f32, bf16 = jnp.float32, jnp.bfloat16
loss_scale = 64.0

NZ, NG, NY, NX = 16, 8, 4, 4
LOW = 512
HIGH = 65536 // LOW
COLS = 6
FAN = 25
CLASSES = 153
LOSS_LANE = 200
FIN_ROWS = 24
SPAN = 128
VMEM = pltpu.VMEM

SEMS = {}
total_sems = 0
for stage, slots in (
    ("w_g", NG), ("aux", NG), ("w_z", NZ), ("x_z", NZ), ("x_g", NG), ("xg", NG), ("lr", NG), ("gl", NG),
    ("gp", NZ), ("rs", NZ), ("y1", NY), ("fz", NZ), ("fx", NX), ("fc", 2), ("dw", NG), ("y2", NY),
):
    SEMS[stage] = total_sems
    total_sems += slots


def dot(a, b, ca=1, cb=0):
    return lax.dot_general(a, b, (((ca,), (cb,)), ((), ())), preferred_element_type=f32)


def iota(shape, dim):
    return lax.broadcasted_iota(jnp.int32, shape, dim)


def step_kernel(
    feat, self_ids, nbr_ids, nbr_counts, w1s, w1n, bias1, w2s, w2n, bias2, labels, top_ids, top_counts,
    loss_out, g1s_out, g1n_out, gb1_out, g2s_out, g2n_out, gb2_out,
    split, table, wt, w_src, w_mid, w_all, aux, rows_t, rows_m, xp, x_src, x_in, x_mid, x_all, xg,
    lp, lr, gl_src, gl_all, gp_src, gp_all, g2, rs, y1, full, dw_src, dw_in, y2, send_sem, recv_sem,
):
    o = lax.axis_index("cols")
    y = lax.axis_index("rep")
    z = o // NG
    g = o % NG
    x = g // 2
    c = g % 2

    def to_z(p):
        return {"cols": ((z + p) % NZ) * NG + g, "rep": y}

    def to_g(p):
        return {"cols": z * NG + (g + p) % NG, "rep": y}

    def to_y(p):
        return {"cols": o, "rep": (y + p) % NY}

    def to_x(p):
        return {"cols": z * NG + ((x + p) % NX) * 2 + c, "rep": y}

    def copy(stage, p, src, dst, device):
        at = SEMS[stage] + p
        return pltpu.make_async_remote_copy(
            src_ref=src, dst_ref=dst, send_sem=send_sem.at[at], recv_sem=recv_sem.at[at], device_id=device
        )

    def each(n, body):
        def run(p, carry):
            body(p)
            return carry
        lax.fori_loop(1, n, run, 0)

    barrier = pltpu.get_barrier_semaphore()
    each(NZ, lambda p: pl.semaphore_signal(barrier, inc=1, device_id=to_z(p)))
    each(NG, lambda p: pl.semaphore_signal(barrier, inc=1, device_id=to_g(p)))
    each(NY, lambda p: pl.semaphore_signal(barrier, inc=1, device_id=to_y(p)))

    wt[...] = jnp.zeros_like(wt)
    wt[0:COLS, :] = w1s[...].astype(f32)
    wt[COLS:2 * COLS, :] = w1n[...].astype(f32)
    for d in range(NG):
        w_src[d] = wt[:, d * SPAN:(d + 1) * SPAN].astype(bf16)
    w_mid[g] = w_src[g]

    eye = iota((8, 8), 0) == iota((8, 8), 1)

    def column(ref):
        return jnp.sum(jnp.where(eye, jnp.broadcast_to(ref[...].astype(f32), (8, 8)), 0.0), axis=1, keepdims=True)

    count_col = column(top_counts)
    label_col = column(labels)
    picks = top_ids[...]
    live_top = iota(picks.shape, 1).astype(f32) < count_col
    lane = iota((8, SPAN), 1)
    mine = jnp.where(lane == 8, count_col, jnp.where(lane == 9, label_col, 0.0))
    for s in range(8):
        n_s = jnp.sum(jnp.where(live_top & (picks == s), 1.0, 0.0), axis=1, keepdims=True)
        mine = jnp.where(lane == s, n_s, mine)
    aux[g] = mine

    pl.semaphore_wait(barrier, NZ + NG + NY - 3)

    each(NG, lambda p: copy("w_g", p, w_src.at[(g + p) % NG], w_mid.at[g], to_g(p)).start())
    each(NG, lambda p: copy("aux", p, aux.at[g], aux.at[g], to_g(p)).start())

    def split_high(h, carry):
        piece = feat[:, pl.ds(pl.multiple_of(h * LOW, LOW), LOW)].astype(f32)
        for q in range(LOW // SPAN):
            split[q, pl.ds(pl.multiple_of(h * 8, 8), COLS), :] = piece[:, q * SPAN:(q + 1) * SPAN]
        return carry

    lax.fori_loop(0, HIGH, split_high, 0, unroll=8)
    for k in range(COLS):
        for q in range(LOW // SPAN):
            table[k * HIGH:(k + 1) * HIGH, q * SPAN:(q + 1) * SPAN] = split[q, pl.ds(k, HIGH, stride=8), :].astype(bf16)

    each(NG, lambda p: copy("w_g", p, w_src.at[(g + p) % NG], w_mid.at[(g + NG - p) % NG], to_g(p)).wait_recv())
    w_all[z] = w_mid[...].reshape(SPAN, SPAN)
    each(NZ, lambda p: copy("w_z", p, w_all.at[z], w_all.at[z], to_z(p)).start())

    io_low = iota((LOW, SPAN), 0)
    io_high = iota((HIGH, SPAN), 0)
    counts = nbr_counts[...]

    def look(ids, alive):
        low = jnp.bitwise_and(ids, LOW - 1)
        high = jnp.where(alive, jnp.right_shift(ids, LOW.bit_length() - 1), -1)
        hot = jnp.concatenate([(io_low == low[j:j + 1, :]).astype(f32).astype(bf16) for j in range(8)], axis=1)
        mask = jnp.concatenate([io_high == high[j:j + 1, :] for j in range(8)], axis=1)
        got = dot(table[...], hot)
        return tuple(
            jnp.sum(jnp.where(mask, got[k * HIGH:(k + 1) * HIGH], 0.0).reshape(HIGH // 8, 8, 8 * SPAN), axis=0)
            for k in range(COLS)
        )

    own = look(self_ids[...], counts > 0)

    def add_nbr(k, sums):
        return tuple(a + b for a, b in zip(sums, look(nbr_ids[k], counts > k)))

    sums = lax.fori_loop(0, FAN, add_nbr, tuple(jnp.zeros((8, 8 * SPAN), f32) for _ in range(COLS)))
    rows_t[...] = jnp.zeros_like(rows_t)
    for j in range(8):
        cut = slice(j * SPAN, (j + 1) * SPAN)
        count = counts[j:j + 1, :].astype(f32)
        for k in range(COLS):
            rows_t[j, k:k + 1, :] = jnp.sum(own[k][:, cut], axis=0, keepdims=True)
            rows_t[j, COLS + k:COLS + k + 1, :] = jnp.sum(sums[k][:, cut], axis=0, keepdims=True) / count
    for j in range(8):
        rows_m[pl.ds(j, SPAN, stride=8), :] = rows_t[j].T
    for t in range(8):
        xp[t] = rows_m[t * SPAN:(t + 1) * SPAN, :].T[0:16, :].astype(bf16)

    odd = z % 2
    half = iota((16, SPAN), 1) // 64
    for t in range(8):
        straight = xp[t].astype(f32)
        turned = pltpu.roll(straight, 64, 1)
        x_src[2 * t] = jnp.where(half == odd, jnp.where(odd == 0, straight, turned), 0.0).astype(bf16)
        x_src[2 * t + 1] = jnp.where(half == odd, jnp.where(odd == 1, straight, turned), 0.0).astype(bf16)
    each(NZ, lambda p: copy("x_z", p, x_src.at[(z + p) % NZ], x_in.at[z], to_z(p)).start())
    x_in[z] = x_src[z]
    xg[g] = xp[...]
    each(NZ, lambda p: copy("x_z", p, x_src.at[(z + p) % NZ], x_in.at[(z + NZ - p) % NZ], to_z(p)).wait_recv())
    for t in range(8):
        x_mid[t] = x_in[2 * t] + x_in[2 * t + 1]
    each(NG, lambda p: copy("x_g", p, x_mid, x_all.at[g], to_g(p)).start())
    each(NG, lambda p: copy("xg", p, xp, xg.at[g], to_g(p)).start())
    x_all[g] = x_mid[...]

    each(NG, lambda p: copy("aux", p, aux.at[g], aux.at[(g + NG - p) % NG], to_g(p)).wait_recv())
    lists = aux[...].reshape(64, SPAN)
    top_div = lists[:, 8:9]
    spread = (iota((SPAN, 64), 0) == iota((SPAN, 64), 1) % 8).astype(f32).astype(bf16)
    same = iota((64, 64), 0) // 8 == iota((64, 64), 1) // 8
    picked = jnp.where(same, dot(lists.astype(bf16), spread), 0.0).astype(bf16)

    each(NZ, lambda p: copy("w_z", p, w_all.at[z], w_all.at[(z + NZ - p) % NZ], to_z(p)).wait_recv())
    each(NG, lambda p: copy("x_g", p, x_mid, x_all.at[(g + NG - p) % NG], to_g(p)).wait_recv())

    both = jnp.zeros((SPAN, 2 * SPAN), f32)
    for t in range(8):
        left = x_all[:, t].reshape(SPAN, SPAN)
        right = jnp.concatenate([w_all[2 * t], w_all[2 * t + 1]], axis=1)
        both = both + dot(left, right, 0, 0)
    pre = both[0:64, 0:SPAN] + both[64:SPAN, SPAN:] + bias1[pl.ds(g, 1), :]
    hidden = jnp.maximum(pre, 0.0).astype(bf16)
    top_mean = (dot(picked, hidden) / top_div).astype(bf16)
    span = pl.ds(pl.multiple_of(g * SPAN, SPAN), SPAN)
    w2s_g = w2s[:, span]
    w2n_g = w2n[:, span]
    part = dot(hidden, w2s_g, 1, 1) + dot(top_mean, w2n_g, 1, 1)
    lp[...] = jnp.zeros_like(lp)
    lp[:, :, 0:CLASSES] = part.reshape(NG, 8, CLASSES)
    each(NG, lambda p: copy("lr", p, lp.at[(g + p) % NG], lr.at[g], to_g(p)).start())
    lr[g] = lp[g]
    each(NG, lambda p: copy("lr", p, lp.at[(g + p) % NG], lr.at[(g + NG - p) % NG], to_g(p)).wait_recv())

    logits = jnp.sum(lr[...], axis=0)[:, 0:CLASSES] + bias2[...]
    exps = jnp.exp(logits)
    total = jnp.sum(exps, axis=1, keepdims=True)
    onehot = jnp.where(iota((8, CLASSES), 1).astype(f32) == label_col, 1.0, 0.0)
    row_loss = jnp.log(total) - jnp.sum(onehot * logits, axis=1, keepdims=True)
    targets = 8 * NG * NZ * NY
    grad = ((exps / total - onehot) * (loss_scale / targets)).astype(bf16)
    gl_src[...] = jnp.where(iota((8, 2 * SPAN), 1) == LOSS_LANE, row_loss, 0.0)
    gl_src[:, 0:CLASSES] = grad.astype(f32)
    each(NG, lambda p: copy("gl", p, gl_src, gl_all.at[g], to_g(p)).start())
    gl_all[g] = gl_src[...]
    each(NG, lambda p: copy("gl", p, gl_src, gl_all.at[(g + NG - p) % NG], to_g(p)).wait_recv())

    gl_rows = gl_all[...].reshape(64, 2 * SPAN)
    gl = gl_rows[:, 0:CLASSES].astype(bf16)
    back_top = dot(gl, w2n_g) / top_div
    top_1 = back_top.astype(bf16)
    rest = back_top - top_1.astype(f32)
    top_2 = rest.astype(bf16)
    top_3 = (rest - top_2.astype(f32)).astype(bf16)
    back = dot(gl, w2s_g) + (dot(picked, top_1, 0, 0) + (dot(picked, top_2, 0, 0) + dot(picked, top_3, 0, 0)))
    grad_pre = jnp.where(pre > 0.0, back, 0.0).astype(bf16)
    gp_src[...] = grad_pre
    each(NZ, lambda p: copy("gp", p, gp_src, gp_all.at[z], to_z(p)).start())
    gp_all[z] = gp_src[...]

    g2[...] = jnp.zeros_like(g2)
    g2[0:CLASSES, :] = dot(gl, hidden, 0, 0)
    g2[160:160 + CLASSES, :] = dot(gl, top_mean, 0, 0)
    g2[320:321, :] = jnp.sum(grad_pre.astype(f32), axis=0, keepdims=True)
    col_sums = jnp.sum(gl_rows, axis=0, keepdims=True)
    g2[321:322, :] = col_sums[:, 0:SPAN]
    g2[322:323, :] = col_sums[:, SPAN:]

    def block(d):
        return g2.at[pl.ds(pl.multiple_of(d * FIN_ROWS, 8), FIN_ROWS)]

    each(NZ, lambda p: copy("rs", p, block((z + p) % NZ), rs.at[z], to_z(p)).start())
    rs[z] = g2[pl.ds(pl.multiple_of(z * FIN_ROWS, 8), FIN_ROWS), :]

    each(NG, lambda p: copy("xg", p, xp, xg.at[(g + NG - p) % NG], to_g(p)).wait_recv())
    each(NZ, lambda p: copy("gp", p, gp_src, gp_all.at[(z + NZ - p) % NZ], to_z(p)).wait_recv())
    dw = jnp.zeros((SPAN, SPAN), f32)
    for t in range(8):
        dw = dw + dot(xg[:, t].reshape(SPAN, SPAN), gp_all[2 * t:2 * t + 2].reshape(SPAN, SPAN))
    dw_src[...] = dw.reshape(NG, 16, SPAN)
    each(NG, lambda p: copy("dw", p, dw_src.at[(g + p) % NG], dw_in.at[g], to_g(p)).start())
    dw_in[g] = dw_src[g]

    each(NZ, lambda p: copy("rs", p, block((z + p) % NZ), rs.at[(z + NZ - p) % NZ], to_z(p)).wait_recv())
    y1[y] = jnp.sum(rs[...], axis=0)
    each(NY, lambda p: copy("y1", p, y1.at[y], y1.at[y], to_y(p)).start())

    each(NG, lambda p: copy("dw", p, dw_src.at[(g + p) % NG], dw_in.at[(g + NG - p) % NG], to_g(p)).wait_recv())
    y2[y] = dw_in[...]
    each(NY, lambda p: copy("y2", p, y2.at[y], y2.at[y], to_y(p)).start())

    each(NY, lambda p: copy("y1", p, y1.at[y], y1.at[(y + NY - p) % NY], to_y(p)).wait_recv())
    fin = jnp.sum(y1[...], axis=0)
    fin_16 = fin.astype(bf16)
    low_part = (fin[8:16] - fin_16[8:16].astype(f32)).astype(bf16)
    full[c, x, z] = jnp.concatenate([fin_16.astype(f32), low_part.astype(f32)], axis=0).astype(bf16)
    here = full.at[c, x, z]
    each(NZ, lambda p: copy("fz", p, here, here, to_z(p)).start())

    each(NY, lambda p: copy("y2", p, y2.at[y], y2.at[(y + NY - p) % NY], to_y(p)).wait_recv())
    g1 = jnp.sum(y2[...], axis=0)
    for d in range(NG):
        g1s_out[:, d * SPAN:(d + 1) * SPAN] = g1[d, 0:COLS]
        g1n_out[:, d * SPAN:(d + 1) * SPAN] = g1[d, COLS:2 * COLS]

    each(NZ, lambda p: copy("fz", p, here, full.at[c, x, (z + NZ - p) % NZ], to_z(p)).wait_recv())
    column_x = full.at[c, x]
    each(NX, lambda p: copy("fx", p, column_x, column_x, to_x(p)).start())
    each(NX, lambda p: copy("fx", p, column_x, full.at[c, (x + NX - p) % NX], to_x(p)).wait_recv())
    to_core = {"cols": z * NG + x * 2 + (1 - c), "rep": y}
    copy("fc", 0, full.at[c], full.at[c], to_core).start()
    copy("fc", 0, full.at[c], full.at[1 - c], to_core).wait_recv()

    for d in range(NG):
        got = full[d % 2, d // 2].astype(f32)
        flat = got[:, 0:FIN_ROWS].reshape(NZ * FIN_ROWS, SPAN)
        cut = slice(d * SPAN, (d + 1) * SPAN)
        g2s_out[:, cut] = flat[0:CLASSES]
        g2n_out[:, cut] = flat[160:160 + CLASSES]
        tail = flat[320:328] + got[13, 24:32]
        gb1_out[d:d + 1, :] = tail[0:1]
        if d == 0:
            gb2_out[:, 0:SPAN] = tail[1:2]
            gb2_out[:, SPAN:CLASSES] = tail[2:3, 0:CLASSES - SPAN]
            loss_out[...] = tail[2:3, LOSS_LANE - SPAN:LOSS_LANE - SPAN + 1] / targets

    each(NG, lambda p: copy("w_g", p, w_src.at[(g + p) % NG], w_mid.at[g], to_g(p)).wait_send())
    each(NG, lambda p: copy("aux", p, aux.at[g], aux.at[g], to_g(p)).wait_send())
    each(NZ, lambda p: copy("w_z", p, w_all.at[z], w_all.at[z], to_z(p)).wait_send())
    each(NZ, lambda p: copy("x_z", p, x_src.at[(z + p) % NZ], x_in.at[z], to_z(p)).wait_send())
    each(NG, lambda p: copy("x_g", p, x_mid, x_all.at[g], to_g(p)).wait_send())
    each(NG, lambda p: copy("xg", p, xp, xg.at[g], to_g(p)).wait_send())
    each(NG, lambda p: copy("lr", p, lp.at[(g + p) % NG], lr.at[g], to_g(p)).wait_send())
    each(NG, lambda p: copy("gl", p, gl_src, gl_all.at[g], to_g(p)).wait_send())
    each(NZ, lambda p: copy("gp", p, gp_src, gp_all.at[z], to_z(p)).wait_send())
    each(NZ, lambda p: copy("rs", p, block((z + p) % NZ), rs.at[z], to_z(p)).wait_send())
    each(NG, lambda p: copy("dw", p, dw_src.at[(g + p) % NG], dw_in.at[g], to_g(p)).wait_send())
    each(NY, lambda p: copy("y1", p, y1.at[y], y1.at[y], to_y(p)).wait_send())
    each(NY, lambda p: copy("y2", p, y2.at[y], y2.at[y], to_y(p)).wait_send())
    each(NZ, lambda p: copy("fz", p, here, here, to_z(p)).wait_send())
    each(NX, lambda p: copy("fx", p, column_x, column_x, to_x(p)).wait_send())
    copy("fc", 0, full.at[c], full.at[c], to_core).wait_send()


def per_device(
    features, self_ids, nbr_ids, nbr_counts, w1_self, w1_nbr, bias1, w2_self, w2_nbr, bias2, labels, top_ids, top_counts
):
    hidden = bias1.shape[0]
    shapes = (
        ((1, 1), f32), ((COLS, hidden), f32), ((COLS, hidden), f32), ((NG, SPAN), f32),
        ((CLASSES, hidden), f32), ((CLASSES, hidden), f32), ((1, CLASSES), f32),
    )
    scratch = [
        VMEM((LOW // SPAN, HIGH * 8, SPAN), f32),
        VMEM((HIGH * COLS, LOW), bf16),
        VMEM((16, hidden), f32),
        VMEM((NG, 16, SPAN), bf16),
        VMEM((NG, 16, SPAN), bf16),
        VMEM((NZ, SPAN, SPAN), bf16),
        VMEM((NG, 8, SPAN), f32),
        VMEM((8, SPAN, SPAN), f32),
        VMEM((8 * SPAN, SPAN), f32),
        VMEM((8, 16, SPAN), bf16),
        VMEM((NZ, 16, SPAN), bf16),
        VMEM((NZ, 16, SPAN), bf16),
        VMEM((8, 16, SPAN), bf16),
        VMEM((NG, 8, 16, SPAN), bf16),
        VMEM((NG, 8, 16, SPAN), bf16),
        VMEM((NG, 8, 2 * SPAN), f32),
        VMEM((NG, 8, 2 * SPAN), f32),
        VMEM((8, 2 * SPAN), f32),
        VMEM((NG, 8, 2 * SPAN), f32),
        VMEM((64, SPAN), bf16),
        VMEM((NZ, 64, SPAN), bf16),
        VMEM((NZ * FIN_ROWS, SPAN), f32),
        VMEM((NZ, FIN_ROWS, SPAN), f32),
        VMEM((NY, FIN_ROWS, SPAN), f32),
        VMEM((2, NX, NZ, 32, SPAN), bf16),
        VMEM((NG, 16, SPAN), f32),
        VMEM((NG, 16, SPAN), f32),
        VMEM((NY, NG, 16, SPAN), f32),
        pltpu.SemaphoreType.DMA((total_sems,)),
        pltpu.SemaphoreType.DMA((total_sems,)),
    ]
    loss, g1s, g1n, gb1, g2s, g2n, gb2 = pl.pallas_call(
        step_kernel,
        out_shape=[jax.ShapeDtypeStruct(s, t) for s, t in shapes],
        in_specs=[pl.BlockSpec(memory_space=VMEM)] * 13,
        out_specs=[pl.BlockSpec(memory_space=VMEM)] * 7,
        scratch_shapes=scratch,
        compiler_params=pltpu.CompilerParams(
            collective_id=0, has_side_effects=True, vmem_limit_bytes=48 * 2**20
        ),
        name="step",
    )(
        features.T, self_ids.T, jnp.transpose(nbr_ids, (2, 1, 0)), nbr_counts.T, w1_self, w1_nbr,
        bias1.reshape(NG, SPAN), w2_self.T, w2_nbr.T, bias2.reshape(1, CLASSES), labels.reshape(1, 8),
        top_ids, top_counts.reshape(1, 8),
    )
    return loss.reshape(()), g1s, g1n, gb1.reshape(hidden), g2s.T, g2n.T, gb2.reshape(CLASSES)


def solution(mesh):
    in_specs = (
        P(None, "cols"), P(None, "rep"), P(None, "rep", None), P(None, "rep"), P("cols", None), P("cols", None),
        P(), P(), P(), P(), P(("cols", "rep")), P(("cols", "rep"), None), P(("cols", "rep")),
    )
    out_specs = (P(), P("cols", None), P("cols", None), P(), P(), P(), P())
    return jax.shard_map(per_device, mesh=mesh, in_specs=in_specs, out_specs=out_specs, check_vma=False)
```

```python
import jax
import jax.numpy as jnp
from jax import lax
from jax.experimental import pallas as pl
from jax.experimental.pallas import tpu as pltpu
from jax.sharding import PartitionSpec as P

f32, bf16 = jnp.float32, jnp.bfloat16
loss_scale = 64.0

NZ, NG, NY, NX = 16, 8, 4, 4
TARGETS = 8 * NZ * NG * NY
LOW = 512
HIGH = 65536 // LOW
COLS = 6
FAN = 25
CLASSES = 153
LOSS_LANE = 200
SPAN = 128
NP = NX * NY
NBR_AT = 159
TAIL_AT = 312
GRAD_ROWS = 320
PART = GRAD_ROWS // NY
TILES = PART // 8
VMEM = pltpu.VMEM

SEMS = {}
total_sems = 0
for stage, slots in (
    ("w_g", NG), ("aux", NG), ("w_z", NZ), ("x_z", NZ), ("x_g", NG), ("xg", NG), ("lr", NG), ("gl", NG),
    ("gp_far", 4), ("gp_near", 4), ("ry", NY), ("rz", NZ), ("az", NZ), ("plane", NP), ("core", NP),
    ("dw", NG), ("y2", NY),
):
    SEMS[stage] = total_sems
    total_sems += slots


def dot(a, b, ca=1, cb=0):
    return lax.dot_general(a, b, (((ca,), (cb,)), ((), ())), preferred_element_type=f32)


def iota(shape, dim):
    return lax.broadcasted_iota(jnp.int32, shape, dim)


def step_kernel(
    feat_hbm, self_hbm, nbr_hbm, counts_hbm, w1s_hbm, w1n_hbm, bias1_hbm, w2s_hbm, w2n_hbm, bias2_hbm, labels_hbm,
    top_hbm, top_counts_hbm, full, g1_out,
    feat, self_ids, nbr_ids, nbr_counts, w1s, w1n, bias1, w2s, w2n, bias2, labels, top_ids, top_counts,
    split, table, wt, w_src, w_mid, w_all, aux, rows_t, rows_m, xp, x_src, x_in, x_mid, x_all, xg,
    lp, lr, gl_src, gl_all, gp_all, g2, ra, r1, rb, rc, dw_src, dw_in, y2, send_sem, recv_sem, load_sem,
):
    o = lax.axis_index("cols")
    y = lax.axis_index("rep")
    z = o // NG
    g = o % NG
    x = g // 2
    c = g % 2
    here = x * NY + y

    def to_z(p):
        return {"cols": ((z + p) % NZ) * NG + g, "rep": y}

    def to_g(p):
        return {"cols": z * NG + (g + p) % NG, "rep": y}

    def to_y(p):
        return {"cols": o, "rep": (y + p) % NY}

    def to_plane(p):
        q = (here + p) % NP
        return {"cols": z * NG + (q // NY) * 2 + c, "rep": q % NY}

    to_core = {"cols": z * NG + x * 2 + (1 - c), "rep": y}

    def copy(stage, p, src, dst, device):
        at = SEMS[stage] + p
        return pltpu.make_async_remote_copy(
            src_ref=src, dst_ref=dst, send_sem=send_sem.at[at], recv_sem=recv_sem.at[at], device_id=device
        )

    def each(n, body, first=1):
        def run(p, carry):
            body(p)
            return carry
        lax.fori_loop(first, n, run, 0)

    loads = [
        pltpu.make_async_copy(src, dst, load_sem.at[i])
        for i, (src, dst) in enumerate((
            (w1s_hbm, w1s), (w1n_hbm, w1n), (top_counts_hbm, top_counts), (labels_hbm, labels), (top_hbm, top_ids),
            (feat_hbm, feat), (self_hbm, self_ids), (counts_hbm, nbr_counts), (nbr_hbm, nbr_ids),
            (bias1_hbm, bias1), (bias2_hbm, bias2), (w2s_hbm, w2s), (w2n_hbm, w2n),
        ))
    ]
    for load in loads:
        load.start()

    barrier = pltpu.get_barrier_semaphore()
    each(NZ, lambda p: pl.semaphore_signal(barrier, inc=1, device_id=to_z(p)))
    each(NG, lambda p: pl.semaphore_signal(barrier, inc=1, device_id=to_g(p)))

    def signal_plane(p):
        device = {"cols": z * NG + (p // (NY - 1)) * 2 + c, "rep": (y + 1 + p % (NY - 1)) % NY}
        pl.semaphore_signal(barrier, inc=1, device_id=device)

    each(NX * (NY - 1), signal_plane, 0)

    with jax.named_scope("prepare"):
        wt[...] = jnp.zeros_like(wt)
        for load in loads[0:5]:
            load.wait()
        wt[0:COLS, :] = w1s[...].astype(f32)
        wt[COLS:2 * COLS, :] = w1n[...].astype(f32)
        for d in range(NG):
            w_src[d] = wt[:, d * SPAN:(d + 1) * SPAN].astype(bf16)
        w_mid[g] = w_src[g]

        eye = iota((8, 8), 0) == iota((8, 8), 1)

        def column(ref):
            return jnp.sum(jnp.where(eye, jnp.broadcast_to(ref[...].astype(f32), (8, 8)), 0.0), axis=1, keepdims=True)

        count_col = column(top_counts)
        label_col = column(labels)
        picks = top_ids[...]
        live_top = iota(picks.shape, 1).astype(f32) < count_col
        lane = iota((8, SPAN), 1)
        mine = jnp.where(lane == 8, count_col, jnp.where(lane == 9, label_col, 0.0))
        for s in range(8):
            n_s = jnp.sum(jnp.where(live_top & (picks == s), 1.0, 0.0), axis=1, keepdims=True)
            mine = jnp.where(lane == s, n_s, mine)
        aux[g] = mine

    with jax.named_scope("barrier"):
        pl.semaphore_wait(barrier, NZ - 1 + NG - 1 + NX * (NY - 1))

    each(NG, lambda p: copy("w_g", p, w_src.at[(g + p) % NG], w_mid.at[g], to_g(p)).start())
    each(NG, lambda p: copy("aux", p, aux.at[g], aux.at[g], to_g(p)).start())

    with jax.named_scope("table"):
        loads[5].wait()

        def split_high(h, carry):
            piece = feat[:, pl.ds(pl.multiple_of(h * LOW, LOW), LOW)].astype(f32)
            for q in range(LOW // SPAN):
                split[q, pl.ds(pl.multiple_of(h * 8, 8), COLS), :] = piece[:, q * SPAN:(q + 1) * SPAN]
            return carry

        lax.fori_loop(0, HIGH, split_high, 0, unroll=8)
        for k in range(COLS):
            for q in range(LOW // SPAN):
                table[k * HIGH:(k + 1) * HIGH, q * SPAN:(q + 1) * SPAN] = (
                    split[q, pl.ds(k, HIGH, stride=8), :].astype(bf16)
                )

    with jax.named_scope("weights"):
        each(NG, lambda p: copy("w_g", p, w_src.at[(g + p) % NG], w_mid.at[(g + NG - p) % NG], to_g(p)).wait_recv())
        w_all[z] = w_mid[...].reshape(SPAN, SPAN)
        each(NZ, lambda p: copy("w_z", p, w_all.at[z], w_all.at[z], to_z(p)).start())

    with jax.named_scope("lookup"):
        for load in loads[6:9]:
            load.wait()
        io_low = iota((LOW, SPAN), 0)
        io_high = iota((HIGH, SPAN), 0)
        counts = nbr_counts[...]

        def look(ids, alive):
            low = jnp.bitwise_and(ids, LOW - 1)
            high = jnp.where(alive, jnp.right_shift(ids, LOW.bit_length() - 1), -1)
            hot = jnp.concatenate([(io_low == low[j:j + 1, :]).astype(f32).astype(bf16) for j in range(8)], axis=1)
            mask = jnp.concatenate([io_high == high[j:j + 1, :] for j in range(8)], axis=1)
            got = dot(table[...], hot)
            return tuple(
                jnp.sum(jnp.where(mask, got[k * HIGH:(k + 1) * HIGH], 0.0).reshape(HIGH // 8, 8, 8 * SPAN), axis=0)
                for k in range(COLS)
            )

        own = look(self_ids[...], counts > 0)

        def add_nbr(k, sums):
            return tuple(a + b for a, b in zip(sums, look(nbr_ids[k], counts > k)))

        sums = lax.fori_loop(0, FAN, add_nbr, tuple(jnp.zeros((8, 8 * SPAN), f32) for _ in range(COLS)), unroll=5)

    with jax.named_scope("rows"):
        rows_t[...] = jnp.zeros_like(rows_t)
        for j in range(8):
            cut = slice(j * SPAN, (j + 1) * SPAN)
            count = counts[j:j + 1, :].astype(f32)
            for k in range(COLS):
                rows_t[j, k:k + 1, :] = jnp.sum(own[k][:, cut], axis=0, keepdims=True)
                rows_t[j, COLS + k:COLS + k + 1, :] = jnp.sum(sums[k][:, cut], axis=0, keepdims=True) / count
            rows_t[j, 2 * COLS:2 * COLS + 1, :] = jnp.ones((1, SPAN), f32)
        for j in range(8):
            rows_m[pl.ds(j, SPAN, stride=8), :] = rows_t[j].T
        for t in range(8):
            xp[t] = rows_m[t * SPAN:(t + 1) * SPAN, :].T[0:16, :].astype(bf16)

        odd = z % 2
        half = iota((16, SPAN), 1) // 64
        for t in range(8):
            straight = xp[t].astype(f32)
            turned = pltpu.roll(straight, 64, 1)
            x_src[2 * t] = jnp.where(half == odd, jnp.where(odd == 0, straight, turned), 0.0).astype(bf16)
            x_src[2 * t + 1] = jnp.where(half == odd, jnp.where(odd == 1, straight, turned), 0.0).astype(bf16)
        each(NZ, lambda p: copy("x_z", p, x_src.at[(z + p) % NZ], x_in.at[z], to_z(p)).start())
        x_in[z] = x_src[z]
        xg[g] = xp[...]

    with jax.named_scope("lists"):
        each(NG, lambda p: copy("aux", p, aux.at[g], aux.at[(g + NG - p) % NG], to_g(p)).wait_recv())
        lists = aux[...].reshape(64, SPAN)
        top_div = lists[:, 8:9]
        spread = (iota((SPAN, 64), 0) == iota((SPAN, 64), 1) % 8).astype(f32).astype(bf16)
        same = iota((64, 64), 0) // 8 == iota((64, 64), 1) // 8
        picked = jnp.where(same, dot(lists.astype(bf16), spread), 0.0).astype(bf16)
        for load in loads[9:]:
            load.wait()

    with jax.named_scope("rows_to_z"):
        each(NZ, lambda p: copy("x_z", p, x_src.at[(z + p) % NZ], x_in.at[(z + NZ - p) % NZ], to_z(p)).wait_recv())
    for t in range(8):
        x_mid[t] = x_in[2 * t] + x_in[2 * t + 1]
    each(NG, lambda p: copy("x_g", p, x_mid, x_all.at[g], to_g(p)).start())
    each(NG, lambda p: copy("xg", p, xp, xg.at[g], to_g(p)).start())
    x_all[g] = x_mid[...]

    with jax.named_scope("weights_over_z"):
        each(NZ, lambda p: copy("w_z", p, w_all.at[z], w_all.at[(z + NZ - p) % NZ], to_z(p)).wait_recv())
    with jax.named_scope("rows_over_g"):
        each(NG, lambda p: copy("x_g", p, x_mid, x_all.at[(g + NG - p) % NG], to_g(p)).wait_recv())

    with jax.named_scope("layers"):
        both = jnp.zeros((SPAN, 2 * SPAN), f32)
        for t in range(8):
            left = x_all[:, t].reshape(SPAN, SPAN)
            right = jnp.concatenate([w_all[2 * t], w_all[2 * t + 1]], axis=1)
            both = both + dot(left, right, 0, 0)
        pre = both[0:64, 0:SPAN] + both[64:SPAN, SPAN:] + bias1[pl.ds(g, 1), :]
        hidden = jnp.maximum(pre, 0.0).astype(bf16)
        top_mean = (dot(picked, hidden) / top_div).astype(bf16)
        span = pl.ds(pl.multiple_of(g * SPAN, SPAN), SPAN)
        w2s_g = w2s[:, span]
        w2n_g = w2n[:, span]
        part = dot(hidden, w2s_g, 1, 1) + dot(top_mean, w2n_g, 1, 1)
        lp[...] = jnp.zeros_like(lp)
        lp[:, :, 0:CLASSES] = part.reshape(NG, 8, CLASSES)
        each(NG, lambda p: copy("lr", p, lp.at[(g + p) % NG], lr.at[g], to_g(p)).start())
        lr[g] = lp[g]
    with jax.named_scope("logits_wait"):
        each(NG, lambda p: copy("lr", p, lp.at[(g + p) % NG], lr.at[(g + NG - p) % NG], to_g(p)).wait_recv())

    with jax.named_scope("softmax"):
        logits = jnp.sum(lr[...], axis=0)[:, 0:CLASSES] + bias2[...]
        exps = jnp.exp(logits)
        total = jnp.sum(exps, axis=1, keepdims=True)
        onehot = jnp.where(iota((8, CLASSES), 1).astype(f32) == label_col, 1.0, 0.0)
        row_loss = jnp.log(total) - jnp.sum(onehot * logits, axis=1, keepdims=True)
        grad = ((exps / total - onehot) * (loss_scale / TARGETS)).astype(bf16)
        gl_src[...] = jnp.where(iota((8, 2 * SPAN), 1) == LOSS_LANE, row_loss, 0.0)
        gl_src[:, 0:CLASSES] = grad.astype(f32)
        each(NG, lambda p: copy("gl", p, gl_src, gl_all.at[g], to_g(p)).start())
        gl_all[g] = gl_src[...]
        g2[...] = jnp.zeros_like(g2)
    with jax.named_scope("grad_logits_wait"):
        each(NG, lambda p: copy("gl", p, gl_src, gl_all.at[(g + NG - p) % NG], to_g(p)).wait_recv())

    with jax.named_scope("classifier_grads"):
        gl_rows = gl_all[...].reshape(64, 2 * SPAN)
        gl = gl_rows[:, 0:CLASSES].astype(bf16)
        g2[0:CLASSES, :] = dot(gl, hidden, 0, 0)
        g2[NBR_AT:NBR_AT + CLASSES, :] = dot(gl, top_mean, 0, 0)
        col_sums = jnp.sum(gl_rows, axis=0, keepdims=True)
        g2[TAIL_AT:TAIL_AT + 1, :] = col_sums[:, 0:SPAN]
        g2[TAIL_AT + 1:TAIL_AT + 2, :] = col_sums[:, SPAN:]

        def block(d):
            return g2.at[pl.ds(pl.multiple_of(d * PART, 8), PART)]

        each(NY, lambda p: copy("ry", p, block((y + p) % NY), ra.at[y], to_y(p)).start())
        ra[y] = g2[pl.ds(pl.multiple_of(y * PART, 8), PART), :]

    with jax.named_scope("back"):
        back_top = dot(gl, w2n_g) / top_div
        top_1 = back_top.astype(bf16)
        rest = back_top - top_1.astype(f32)
        top_2 = rest.astype(bf16)
        top_3 = (rest - top_2.astype(f32)).astype(bf16)
        back = dot(gl, w2s_g) + (dot(picked, top_1, 0, 0) + (dot(picked, top_2, 0, 0) + dot(picked, top_3, 0, 0)))
        grad_pre = jnp.where(pre > 0.0, back, 0.0).astype(bf16)
        row, col = z % 4, z // 4
        gp_all[row, col] = grad_pre
        mine_gp = gp_all.at[row, col]
        each(4, lambda p: copy("gp_far", p, mine_gp, mine_gp, to_z(4 * p)).start())

    with jax.named_scope("sum_over_rep"):
        each(NY, lambda p: copy("ry", p, block((y + p) % NY), ra.at[(y + NY - p) % NY], to_y(p)).wait_recv())
        r1[...] = jnp.sum(ra[...], axis=0)

        def tile(d):
            return r1.at[pl.ds(pl.multiple_of(d * 8, 8), 8)]

        def send_tile(p):
            d = (z + p) % NZ

            @pl.when(d < TILES)
            def _():
                copy("rz", p, tile(d), rb.at[z], to_z(p)).start()

        each(NZ, send_tile)

    with jax.named_scope("grad_pre_far"):
        each(4, lambda p: copy("gp_far", p, mine_gp, gp_all.at[row, (col + 4 - p) % 4], to_z(4 * p)).wait_recv())
    four = gp_all.at[row]
    near = (1, NZ - 1, 2)
    for i, p in enumerate(near):
        copy("gp_near", i, four, four, to_z(p)).start()

    with jax.named_scope("scatter_over_z"):
        @pl.when(z < TILES)
        def _():
            rb[z] = r1[pl.ds(pl.multiple_of(z * 8, 8), 8), :]
            each(NZ, lambda p: copy("rz", p, tile(z), rb.at[(z + NZ - p) % NZ], to_z(p)).wait_recv())
            rc[z] = jnp.sum(rb[...], axis=0)
            each(NZ, lambda p: copy("az", p, rc.at[z], rc.at[z], to_z(p)).start())

    with jax.named_scope("grad_pre_near"):
        each(NG, lambda p: copy("xg", p, xp, xg.at[(g + NG - p) % NG], to_g(p)).wait_recv())
        for i, p in enumerate(near):
            copy("gp_near", i, four, gp_all.at[(row + 4 - p % 4) % 4], to_z(p)).wait_recv()
    with jax.named_scope("layer_grads"):
        dw = jnp.zeros((SPAN, SPAN), f32)
        for t in range(8):
            pair = [gp_all[(2 * t + i) % 4, (2 * t + i) // 4] for i in range(2)]
            dw = dw + dot(xg[:, t].reshape(SPAN, SPAN), jnp.concatenate(pair, axis=0))
        dw_src[...] = dw.reshape(NG, 16, SPAN)
        each(NG, lambda p: copy("dw", p, dw_src.at[(g + p) % NG], dw_in.at[g], to_g(p)).start())
        dw_in[g] = dw_src[g]

    with jax.named_scope("gather_over_z"):
        def wait_tile(s, carry):
            @pl.when(s != z)
            def _():
                copy("az", (z + NZ - s) % NZ, rc.at[s], rc.at[s], to_z(1)).wait_recv()
            return carry

        lax.fori_loop(0, TILES, wait_tile, 0)
        fin = rc[...].reshape(PART, SPAN)
        low_part = fin - fin.astype(bf16).astype(f32)
        low_part = jnp.concatenate([low_part[0:2], low_part[0:PART - 2]], axis=0)
        at = iota((PART, SPAN), 0) - (TAIL_AT - (NY - 1) * PART)
        is_low = (y == NY - 1) & (at >= 2) & (at < 4)
        full[c, x, y] = jnp.where(is_low, low_part, fin).astype(bf16)
        out_block = full.at[c, x, y]
        each(NP, lambda p: copy("plane", p, out_block, out_block, to_plane(p)).start())
        copy("core", here, out_block, out_block, to_core).start()

    with jax.named_scope("layer_grads_wait"):
        each(NG, lambda p: copy("dw", p, dw_src.at[(g + p) % NG], dw_in.at[(g + NG - p) % NG], to_g(p)).wait_recv())
        y2[y] = dw_in[...]
        each(NY, lambda p: copy("y2", p, y2.at[y], y2.at[y], to_y(p)).start())

    with jax.named_scope("gather_over_plane"):
        def forward(p):
            q = (here + NP - p) % NP
            there = full.at[c, q // NY, q % NY]
            copy("plane", p, out_block, there, to_plane(p)).wait_recv()
            copy("core", q, there, there, to_core).start()

        each(NP, forward)

    with jax.named_scope("layer_grads_over_rep"):
        each(NY, lambda p: copy("y2", p, y2.at[y], y2.at[(y + NY - p) % NY], to_y(p)).wait_recv())
        g1_out[...] = jnp.sum(y2[...], axis=0)

    with jax.named_scope("gather_over_core"):
        def from_core(q):
            there = full.at[1 - c, q // NY, q % NY]
            copy("core", q, there, there, to_core).wait_recv()

        each(NP, from_core, 0)

    with jax.named_scope("sends"):
        each(NG, lambda p: copy("w_g", p, w_src.at[(g + p) % NG], w_mid.at[g], to_g(p)).wait_send())
        each(NG, lambda p: copy("aux", p, aux.at[g], aux.at[g], to_g(p)).wait_send())
        each(NZ, lambda p: copy("w_z", p, w_all.at[z], w_all.at[z], to_z(p)).wait_send())
        each(NZ, lambda p: copy("x_z", p, x_src.at[(z + p) % NZ], x_in.at[z], to_z(p)).wait_send())
        each(NG, lambda p: copy("x_g", p, x_mid, x_all.at[g], to_g(p)).wait_send())
        each(NG, lambda p: copy("xg", p, xp, xg.at[g], to_g(p)).wait_send())
        each(NG, lambda p: copy("lr", p, lp.at[(g + p) % NG], lr.at[g], to_g(p)).wait_send())
        each(NG, lambda p: copy("gl", p, gl_src, gl_all.at[g], to_g(p)).wait_send())
        each(4, lambda p: copy("gp_far", p, mine_gp, mine_gp, to_z(4 * p)).wait_send())
        for i, p in enumerate(near):
            copy("gp_near", i, four, four, to_z(p)).wait_send()
        each(NY, lambda p: copy("ry", p, block((y + p) % NY), ra.at[y], to_y(p)).wait_send())

        def sent_tile(p):
            d = (z + p) % NZ

            @pl.when(d < TILES)
            def _():
                copy("rz", p, tile(d), rb.at[z], to_z(p)).wait_send()

        each(NZ, sent_tile)

        @pl.when(z < TILES)
        def _():
            each(NZ, lambda p: copy("az", p, rc.at[z], rc.at[z], to_z(p)).wait_send())

        each(NP, lambda p: copy("plane", p, out_block, out_block, to_plane(p)).wait_send())
        each(NP, lambda q: copy("core", q, out_block, out_block, to_core).wait_send(), 0)
        each(NG, lambda p: copy("dw", p, dw_src.at[(g + p) % NG], dw_in.at[g], to_g(p)).wait_send())
        each(NY, lambda p: copy("y2", p, y2.at[y], y2.at[y], to_y(p)).wait_send())


def finish_kernel(full, g1, *refs):
    outs, bufs, sem = refs[0:7], refs[7:14], refs[14]
    loss, g1s, g1n, gb1, g2s, g2n, gb2 = bufs
    for d in range(NG):
        cut = slice(d * SPAN, (d + 1) * SPAN)
        flat = full[d % 2, d // 2].astype(f32).reshape(GRAD_ROWS, SPAN)
        g2s[:, cut] = flat[0:CLASSES]
        g2n[:, cut] = flat[NBR_AT:NBR_AT + CLASSES]
        g1s[:, cut] = g1[d, 0:COLS]
        g1n[:, cut] = g1[d, COLS:2 * COLS]
        gb1[d:d + 1, :] = g1[d, 2 * COLS:2 * COLS + 1]
        if d == 0:
            tail = flat[TAIL_AT:TAIL_AT + 2] + flat[TAIL_AT + 2:TAIL_AT + 4]
            gb2[:, 0:SPAN] = tail[0:1]
            gb2[:, SPAN:CLASSES] = tail[1:2, 0:CLASSES - SPAN]
            loss[...] = tail[1:2, LOSS_LANE - SPAN:LOSS_LANE - SPAN + 1] / TARGETS
    stores = [pltpu.make_async_copy(b, r, sem.at[i]) for i, (b, r) in enumerate(zip(bufs, outs))]
    for store in stores:
        store.start()
    for store in stores:
        store.wait()


def per_device(
    features, self_ids, nbr_ids, nbr_counts, w1_self, w1_nbr, bias1, w2_self, w2_nbr, bias2, labels, top_ids, top_counts
):
    hidden = bias1.shape[0]
    operands = (
        features.T, self_ids.T, jnp.transpose(nbr_ids, (2, 1, 0)), nbr_counts.T, w1_self, w1_nbr,
        bias1.reshape(NG, SPAN), w2_self.T, w2_nbr.T, bias2.reshape(1, CLASSES), labels.reshape(1, 8),
        top_ids, top_counts.reshape(1, 8),
    )
    scratch = [VMEM(a.shape, a.dtype) for a in operands] + [
        VMEM((LOW // SPAN, HIGH * 8, SPAN), f32),
        VMEM((HIGH * COLS, LOW), bf16),
        VMEM((16, hidden), f32),
        VMEM((NG, 16, SPAN), bf16),
        VMEM((NG, 16, SPAN), bf16),
        VMEM((NZ, SPAN, SPAN), bf16),
        VMEM((NG, 8, SPAN), f32),
        VMEM((8, SPAN, SPAN), f32),
        VMEM((8 * SPAN, SPAN), f32),
        VMEM((8, 16, SPAN), bf16),
        VMEM((NZ, 16, SPAN), bf16),
        VMEM((NZ, 16, SPAN), bf16),
        VMEM((8, 16, SPAN), bf16),
        VMEM((NG, 8, 16, SPAN), bf16),
        VMEM((NG, 8, 16, SPAN), bf16),
        VMEM((NG, 8, 2 * SPAN), f32),
        VMEM((NG, 8, 2 * SPAN), f32),
        VMEM((8, 2 * SPAN), f32),
        VMEM((NG, 8, 2 * SPAN), f32),
        VMEM((4, 4, 64, SPAN), bf16),
        VMEM((GRAD_ROWS, SPAN), f32),
        VMEM((NY, PART, SPAN), f32),
        VMEM((PART, SPAN), f32),
        VMEM((NZ, 8, SPAN), f32),
        VMEM((TILES, 8, SPAN), f32),
        VMEM((NG, 16, SPAN), f32),
        VMEM((NG, 16, SPAN), f32),
        VMEM((NY, NG, 16, SPAN), f32),
        pltpu.SemaphoreType.DMA((total_sems,)),
        pltpu.SemaphoreType.DMA((total_sems,)),
        pltpu.SemaphoreType.DMA((len(operands),)),
    ]
    full, g1 = pl.pallas_call(
        step_kernel,
        out_shape=[
            jax.ShapeDtypeStruct((2, NX, NY, PART, SPAN), bf16), jax.ShapeDtypeStruct((NG, 16, SPAN), f32),
        ],
        in_specs=[pl.BlockSpec(memory_space=pltpu.HBM)] * len(operands),
        out_specs=[pl.BlockSpec(memory_space=VMEM)] * 2,
        scratch_shapes=scratch,
        compiler_params=pltpu.CompilerParams(
            collective_id=0, has_side_effects=True, vmem_limit_bytes=60 * 2**20
        ),
        name="step",
    )(*operands)
    shapes = (
        (1, 1), (COLS, hidden), (COLS, hidden), (NG, SPAN), (CLASSES, hidden), (CLASSES, hidden), (1, CLASSES),
    )
    loss, g1s, g1n, gb1, g2s, g2n, gb2 = pl.pallas_call(
        finish_kernel,
        out_shape=[jax.ShapeDtypeStruct(s, f32) for s in shapes],
        in_specs=[pl.BlockSpec(memory_space=VMEM)] * 2,
        out_specs=[pl.BlockSpec(memory_space=pltpu.HBM)] * len(shapes),
        scratch_shapes=[VMEM(s, f32) for s in shapes] + [pltpu.SemaphoreType.DMA((len(shapes),))],
        name="finish",
    )(full, g1)
    return loss.reshape(()), g1s, g1n, gb1.reshape(hidden), g2s.T, g2n.T, gb2.reshape(CLASSES)


def solution(mesh):
    in_specs = (
        P(None, "cols"), P(None, "rep"), P(None, "rep", None), P(None, "rep"), P("cols", None), P("cols", None),
        P(), P(), P(), P(), P(("cols", "rep")), P(("cols", "rep"), None), P(("cols", "rep")),
    )
    out_specs = (P(), P("cols", None), P("cols", None), P(), P(), P(), P())
    return jax.shard_map(per_device, mesh=mesh, in_specs=in_specs, out_specs=out_specs, check_vma=False)
```

```python
import jax
import jax.numpy as jnp
from jax import lax
from jax.experimental import pallas as pl
from jax.experimental.pallas import tpu as pltpu
from jax.sharding import PartitionSpec as P

f32, bf16 = jnp.float32, jnp.bfloat16
loss_scale = 64.0

NZ, NG, NY, NX = 16, 8, 4, 4
TARGETS = 8 * NZ * NG * NY
LOW = 512
HIGH = 65536 // LOW
COLS = 6
FAN = 25
CLASSES = 153
LOSS_LANE = 200
SPAN = 128
NP = NX * NY
NBR_AT = 159
TAIL_AT = 312
GRAD_ROWS = 384
PART = GRAD_ROWS // NY
BLOCK = PART // 4
NEAR = (0, 1, NZ - 1, 2)
VMEM = pltpu.VMEM

SEMS = {}
total_sems = 0
for stage, slots in (
    ("w_g", NG), ("aux", NG), ("w_far", 4), ("w_near", 4), ("x_z", NZ), ("x_g", NG), ("xg", NG), ("lr", NG), ("gl", NG),
    ("gp_far", 4), ("gp_near", 4), ("scatter", 16), ("far", 4), ("near", 4), ("plane", NP), ("core", NP),
    ("dw", NG), ("y2", NY),
):
    SEMS[stage] = total_sems
    total_sems += slots


def dot(a, b, ca=1, cb=0):
    return lax.dot_general(a, b, (((ca,), (cb,)), ((), ())), preferred_element_type=f32)


def iota(shape, dim):
    return lax.broadcasted_iota(jnp.int32, shape, dim)


def step_kernel(
    feat_hbm, self_hbm, nbr_hbm, counts_hbm, w1s_hbm, w1n_hbm, bias1_hbm, w2s_hbm, w2n_hbm, bias2_hbm, labels_hbm,
    top_hbm, top_counts_hbm, full, g1_out,
    feat, self_ids, nbr_ids, nbr_counts, w1s, w1n, bias1, w2s, w2n, bias2, labels, top_ids, top_counts,
    split, table, wt, w_src, w_mid, w_all, aux, rows_t, rows_m, xp, x_src, x_in, x_mid, x_all, xg,
    lp, lr, gl_src, gl_all, gp_all, g2, ra, rb, rc, dw_src, dw_in, y2, send_sem, recv_sem, load_sem,
):
    o = lax.axis_index("cols")
    y = lax.axis_index("rep")
    z = o // NG
    g = o % NG
    x = g // 2
    c = g % 2
    here = x * NY + y

    def to_z(p):
        return {"cols": ((z + p) % NZ) * NG + g, "rep": y}

    def to_g(p):
        return {"cols": z * NG + (g + p) % NG, "rep": y}

    def to_y(p):
        return {"cols": o, "rep": (y + p) % NY}

    def to_plane(p):
        q = (here + p) % NP
        return {"cols": z * NG + (q // NY) * 2 + c, "rep": q % NY}

    to_core = {"cols": z * NG + x * 2 + (1 - c), "rep": y}

    def copy(stage, p, src, dst, device):
        at = SEMS[stage] + p
        return pltpu.make_async_remote_copy(
            src_ref=src, dst_ref=dst, send_sem=send_sem.at[at], recv_sem=recv_sem.at[at], device_id=device
        )

    def each(n, body, first=1):
        def run(p, carry):
            body(p)
            return carry
        lax.fori_loop(first, n, run, 0)

    arrivals, departures = {}, []

    def launch(stage, n, device, src, dst, got):
        def begin(i):
            p = n // 2 + ((i + 1) // 2) * (2 * (i % 2) - 1)
            copy(stage, p, src(p), dst, device(p)).start()

        each(n - 1, begin, 0)
        arrivals[stage] = lambda: each(n, lambda p: copy(stage, p, src(p), got(p), device(p)).wait_recv())
        departures.append(lambda: each(n, lambda p: copy(stage, p, src(p), dst, device(p)).wait_send()))

    def launch_near(stage, src, dst, got):
        steps = list(enumerate(NEAR))[1:]
        for i, p in steps:
            copy(stage, i, src, dst, to_z(p)).start()

        def wait_near():
            for i, p in steps:
                copy(stage, i, src, got((z + NZ - p) % 4), to_z(p)).wait_recv()

        def sent_near():
            for i, p in steps:
                copy(stage, i, src, dst, to_z(p)).wait_send()

        arrivals[stage] = wait_near
        departures.append(sent_near)

    def arrive(stage):
        arrivals.pop(stage)()

    def depart():
        while departures:
            departures.pop(0)()

    def to_far(p):
        return to_z(4 * p)

    row, col = z % 4, z // 4

    def far_of(p):
        return (col + 4 - p) % 4

    def z_of(p):
        return (z + NZ - p) % NZ

    def g_of(p):
        return (g + NG - p) % NG

    def y_of(p):
        return (y + NY - p) % NY

    loads = [
        pltpu.make_async_copy(src, dst, load_sem.at[i])
        for i, (src, dst) in enumerate((
            (w1s_hbm, w1s), (w1n_hbm, w1n), (top_counts_hbm, top_counts), (labels_hbm, labels), (top_hbm, top_ids),
            (feat_hbm, feat), (self_hbm, self_ids), (counts_hbm, nbr_counts), (nbr_hbm, nbr_ids),
            (bias1_hbm, bias1), (bias2_hbm, bias2), (w2s_hbm, w2s), (w2n_hbm, w2n),
        ))
    ]
    for load in loads:
        load.start()
    waiting = list(range(13))

    def ready(first, last):
        for i in range(first, last):
            waiting.remove(i)
            loads[i].wait()

    barrier = pltpu.get_barrier_semaphore()
    each(NZ, lambda p: pl.semaphore_signal(barrier, inc=1, device_id=to_z(p)))
    each(NG, lambda p: pl.semaphore_signal(barrier, inc=1, device_id=to_g(p)))

    def signal_plane(p):
        device = {"cols": z * NG + (p // (NY - 1)) * 2 + c, "rep": (y + 1 + p % (NY - 1)) % NY}
        pl.semaphore_signal(barrier, inc=1, device_id=device)

    each(NX * (NY - 1), signal_plane, 0)
    for step in NEAR[1:] + (NZ - 2,):
        each(NY, lambda p, step=step: pl.semaphore_signal(
            barrier, inc=1, device_id={"cols": ((z + step) % NZ) * NG + g, "rep": (y + p) % NY}
        ))

    with jax.named_scope("prepare"):
        wt[...] = jnp.zeros_like(wt)
        ready(0, 5)
        wt[0:COLS, :] = w1s[...].astype(f32)
        wt[COLS:2 * COLS, :] = w1n[...].astype(f32)
        for d in range(NG):
            w_src[d] = wt[:, d * SPAN:(d + 1) * SPAN].astype(bf16)
        w_mid[g] = w_src[g]

        eye = iota((8, 8), 0) == iota((8, 8), 1)

        def column(ref):
            return jnp.sum(jnp.where(eye, jnp.broadcast_to(ref[...].astype(f32), (8, 8)), 0.0), axis=1, keepdims=True)

        count_col = column(top_counts)
        label_col = column(labels)
        picks = top_ids[...]
        live_top = iota(picks.shape, 1).astype(f32) < count_col
        lane = iota((8, SPAN), 1)
        mine = jnp.where(lane == 8, count_col, jnp.where(lane == 9, label_col, 0.0))
        for s in range(8):
            n_s = jnp.sum(jnp.where(live_top & (picks == s), 1.0, 0.0), axis=1, keepdims=True)
            mine = jnp.where(lane == s, n_s, mine)
        aux[g] = mine

    with jax.named_scope("table"):
        ready(5, 6)

        def split_high(h, carry):
            piece = feat[:, pl.ds(pl.multiple_of(h * LOW, LOW), LOW)].astype(f32)
            for q in range(LOW // SPAN):
                split[q, pl.ds(pl.multiple_of(h * 8, 8), COLS), :] = piece[:, q * SPAN:(q + 1) * SPAN]
            return carry

        lax.fori_loop(0, HIGH, split_high, 0, unroll=8)
        for k in range(COLS):
            for q in range(LOW // SPAN):
                table[k * HIGH:(k + 1) * HIGH, q * SPAN:(q + 1) * SPAN] = (
                    split[q, pl.ds(k, HIGH, stride=8), :].astype(bf16)
                )

    with jax.named_scope("lookup"):
        ready(6, 9)
        io_low = iota((256, SPAN), 0).astype(f32).astype(bf16)
        io_high = iota((HIGH, SPAN), 0)
        counts = nbr_counts[...]

        def look(ids, alive):
            low = jnp.bitwise_and(ids, LOW - 1).astype(f32)
            high = jnp.where(alive, jnp.right_shift(ids, LOW.bit_length() - 1), -1)

            def hot_rows(first, j):
                at = jnp.broadcast_to((low[j:j + 1, :] - first).astype(bf16), (256, SPAN))
                return jnp.where(io_low == at, jnp.bfloat16(1), jnp.bfloat16(0))

            hot = jnp.concatenate([
                jnp.concatenate([hot_rows(float(first), j) for j in range(8)], axis=1) for first in range(0, LOW, 256)
            ], axis=0)
            mask = jnp.concatenate([io_high == high[j:j + 1, :] for j in range(8)], axis=1)
            got = dot(table[...], hot)
            return tuple(
                jnp.sum(jnp.where(mask, got[k * HIGH:(k + 1) * HIGH], 0.0).reshape(HIGH // 8, 8, 8 * SPAN), axis=0)
                for k in range(COLS)
            )

        def add_nbr(k, sums):
            return tuple(a + b for a, b in zip(sums, look(nbr_ids[k], counts > k)))

        own = look(self_ids[...], counts > 0)
        pl.semaphore_wait(barrier, NZ - 1 + NG - 1 + NX * (NY - 1) + 4 * (NY - 1))
        launch("w_g", NG, to_g, lambda p: w_src.at[(g + p) % NG], w_mid.at[g], lambda p: w_mid.at[g_of(p)])
        launch("aux", NG, to_g, lambda p: aux.at[g], aux.at[g], lambda p: aux.at[g_of(p)])
        sums = tuple(jnp.zeros((8, 8 * SPAN), f32) for _ in range(COLS))
        sums = lax.fori_loop(0, 5, add_nbr, sums, unroll=5)
        arrive("w_g")
        w_all[row, col] = w_mid[...].reshape(SPAN, SPAN)
        w_mine = w_all.at[row, col]
        launch("w_far", 4, to_far, lambda p: w_mine, w_mine, lambda p: w_all.at[row, far_of(p)])
        sums = lax.fori_loop(5, 15, add_nbr, sums, unroll=5)
        arrive("w_far")
        launch_near("w_near", w_all.at[row], w_all.at[row], lambda r: w_all.at[r])
        sums = lax.fori_loop(15, FAN, add_nbr, sums, unroll=5)

    with jax.named_scope("rows"):
        rows_t[...] = jnp.zeros_like(rows_t)
        for j in range(8):
            cut = slice(j * SPAN, (j + 1) * SPAN)
            count = counts[j:j + 1, :].astype(f32)
            for k in range(COLS):
                rows_t[j, k:k + 1, :] = jnp.sum(own[k][:, cut], axis=0, keepdims=True)
                rows_t[j, COLS + k:COLS + k + 1, :] = jnp.sum(sums[k][:, cut], axis=0, keepdims=True) / count
            rows_t[j, 2 * COLS:2 * COLS + 1, :] = jnp.ones((1, SPAN), f32)
        for j in range(8):
            rows_m[pl.ds(j, SPAN, stride=8), :] = rows_t[j].T
        for t in range(8):
            xp[t] = rows_m[t * SPAN:(t + 1) * SPAN, :].T[0:16, :].astype(bf16)

        odd = z % 2
        half = iota((16, SPAN), 1) // 64
        for t in range(8):
            straight = xp[t].astype(f32)
            turned = pltpu.roll(straight, 64, 1)
            x_src[2 * t] = jnp.where(half == odd, jnp.where(odd == 0, straight, turned), 0.0).astype(bf16)
            x_src[2 * t + 1] = jnp.where(half == odd, jnp.where(odd == 1, straight, turned), 0.0).astype(bf16)
        launch("x_z", NZ, to_z, lambda p: x_src.at[(z + p) % NZ], x_in.at[z], lambda p: x_in.at[z_of(p)])
        x_in[z] = x_src[z]
        xg[g] = xp[...]

    with jax.named_scope("lists"):
        arrive("aux")
        lists = aux[...].reshape(64, SPAN)
        top_div = lists[:, 8:9]
        spread = (iota((SPAN, 64), 0) == iota((SPAN, 64), 1) % 8).astype(f32).astype(bf16)
        same = iota((64, 64), 0) // 8 == iota((64, 64), 1) // 8
        picked = jnp.where(same, dot(lists.astype(bf16), spread), 0.0).astype(bf16)
        ready(9, 13)

    with jax.named_scope("rows_to_z"):
        arrive("w_near")
        depart()
        arrive("x_z")
    for t in range(8):
        x_mid[t] = x_in[2 * t] + x_in[2 * t + 1]
    launch("x_g", NG, to_g, lambda p: x_mid, x_all.at[g], lambda p: x_all.at[g_of(p)])
    x_all[g] = x_mid[...]

    with jax.named_scope("rows_over_g"):
        arrive("x_g")

    with jax.named_scope("layers"):
        both = jnp.zeros((SPAN, 2 * SPAN), f32)
        for t in range(8):
            left = x_all[:, t].reshape(SPAN, SPAN)
            right = jnp.concatenate([w_all[(2 * t + i) % 4, (2 * t + i) // 4] for i in range(2)], axis=1)
            both = both + dot(left, right, 0, 0)
        pre = both[0:64, 0:SPAN] + both[64:SPAN, SPAN:] + bias1[pl.ds(g, 1), :]
        hidden = jnp.maximum(pre, 0.0).astype(bf16)
        top_mean = (dot(picked, hidden) / top_div).astype(bf16)
        span = pl.ds(pl.multiple_of(g * SPAN, SPAN), SPAN)
        w2s_g = w2s[:, span]
        w2n_g = w2n[:, span]
        part = dot(hidden, w2s_g, 1, 1) + dot(top_mean, w2n_g, 1, 1)
        lp[...] = jnp.zeros_like(lp)
        lp[:, :, 0:CLASSES] = part.reshape(NG, 8, CLASSES)
        launch("lr", NG, to_g, lambda p: lp.at[(g + p) % NG], lr.at[g], lambda p: lr.at[g_of(p)])
        lr[g] = lp[g]
    with jax.named_scope("logits_wait"):
        depart()
        arrive("lr")

    with jax.named_scope("softmax"):
        logits = jnp.sum(lr[...], axis=0)[:, 0:CLASSES] + bias2[...]
        exps = jnp.exp(logits)
        total = jnp.sum(exps, axis=1, keepdims=True)
        onehot = jnp.where(iota((8, CLASSES), 1).astype(f32) == label_col, 1.0, 0.0)
        row_loss = jnp.log(total) - jnp.sum(onehot * logits, axis=1, keepdims=True)
        grad = ((exps / total - onehot) * (loss_scale / TARGETS)).astype(bf16)
        gl_src[...] = jnp.where(iota((8, 2 * SPAN), 1) == LOSS_LANE, row_loss, 0.0)
        gl_src[:, 0:CLASSES] = grad.astype(f32)
        launch("gl", NG, to_g, lambda p: gl_src, gl_all.at[g], lambda p: gl_all.at[g_of(p)])
        gl_all[g] = gl_src[...]
        g2[...] = jnp.zeros_like(g2)
    with jax.named_scope("grad_logits_wait"):
        arrive("gl")

    with jax.named_scope("classifier_grads"):
        gl_rows = gl_all[...].reshape(64, 2 * SPAN)
        gl = gl_rows[:, 0:CLASSES].astype(bf16)
        g2[0:CLASSES, :] = dot(gl, hidden, 0, 0)
        g2[NBR_AT:NBR_AT + CLASSES, :] = dot(gl, top_mean, 0, 0)
        col_sums = jnp.sum(gl_rows, axis=0, keepdims=True)
        g2[TAIL_AT:TAIL_AT + 1, :] = col_sums[:, 0:SPAN]
        g2[TAIL_AT + 1:TAIL_AT + 2, :] = col_sums[:, SPAN:]

        def block(r, d):
            return g2.at[pl.ds(pl.multiple_of((d * 4 + r) * BLOCK, 8), BLOCK)]

        def scatter(act, wait=False):
            for i, p in enumerate(NEAR):
                def run(q, i=i, p=p):
                    device = {"cols": ((z + p) % NZ) * NG + g, "rep": (y + q) % NY}
                    got = ra.at[i, y_of(q)] if wait else ra.at[i, y]
                    act(copy("scatter", i * 4 + q, block((z + p) % 4, (y + q) % NY), got, device))

                each(NY, run, 0 if i else 1)

        scatter(lambda send: send.start())
        departures.append(lambda: scatter(lambda send: send.wait_send()))
        ra[0, y] = g2[pl.ds(pl.multiple_of((y * 4 + row) * BLOCK, 8), BLOCK), :]

    with jax.named_scope("back"):
        back_top = dot(gl, w2n_g) / top_div
        top_1 = back_top.astype(bf16)
        rest = back_top - top_1.astype(f32)
        top_2 = rest.astype(bf16)
        top_3 = (rest - top_2.astype(f32)).astype(bf16)
        back = dot(gl, w2s_g) + (dot(picked, top_1, 0, 0) + (dot(picked, top_2, 0, 0) + dot(picked, top_3, 0, 0)))
        grad_pre = jnp.where(pre > 0.0, back, 0.0).astype(bf16)
        gp_all[row, col] = grad_pre
        mine_gp = gp_all.at[row, col]
        launch("gp_far", 4, to_far, lambda p: mine_gp, mine_gp, lambda p: gp_all.at[row, far_of(p)])
        launch("xg", NG, to_g, lambda p: xp, xg.at[g], lambda p: xg.at[g_of(p)])

    with jax.named_scope("scatter"):
        scatter(lambda send: send.wait_recv(), wait=True)
        rb[col] = jnp.sum(ra[...].reshape(4 * NY, BLOCK, SPAN), axis=0)
        mine_rb = rb.at[col]
        launch("far", 4, to_far, lambda p: mine_rb, mine_rb, lambda p: rb.at[far_of(p)])

    with jax.named_scope("grad_pre_far"):
        arrive("gp_far")
        launch_near("gp_near", gp_all.at[row], gp_all.at[row], lambda r: gp_all.at[r])

    with jax.named_scope("far"):
        arrive("far")
        rc[row] = jnp.sum(rb[...], axis=0)
        launch_near("near", rc.at[row], rc.at[row], lambda r: rc.at[r])

    with jax.named_scope("grad_pre_near"):
        arrive("xg")
        arrive("gp_near")
    with jax.named_scope("layer_grads"):
        dw = jnp.zeros((SPAN, SPAN), f32)
        for t in range(8):
            pair = [gp_all[(2 * t + i) % 4, (2 * t + i) // 4] for i in range(2)]
            dw = dw + dot(xg[:, t].reshape(SPAN, SPAN), jnp.concatenate(pair, axis=0))
        dw_src[...] = dw.reshape(NG, 16, SPAN)
        launch("dw", NG, to_g, lambda p: dw_src.at[(g + p) % NG], dw_in.at[g], lambda p: dw_in.at[g_of(p)])
        dw_in[g] = dw_src[g]

    with jax.named_scope("gather_over_z"):
        arrive("near")
        earlier = departures[:]
        departures.clear()
        fin = rc[...].reshape(PART, SPAN)
        low_part = fin - fin.astype(bf16).astype(f32)
        low_part = jnp.concatenate([low_part[0:2], low_part[0:PART - 2]], axis=0)
        at = iota((PART, SPAN), 0) - (TAIL_AT - (NY - 1) * PART)
        is_low = (y == NY - 1) & (at >= 2) & (at < 4)
        full[c, x, y] = jnp.where(is_low, low_part, fin).astype(bf16)
        out_block = full.at[c, x, y]
        each(NP, lambda p: copy("plane", p, out_block, out_block, to_plane(p)).start())
        departures.append(lambda: each(NP, lambda p: copy("plane", p, out_block, out_block, to_plane(p)).wait_send()))
        copy("core", here, out_block, out_block, to_core).start()

    with jax.named_scope("layer_grads_wait"):
        arrive("dw")
        y2[y] = dw_in[...]
        launch("y2", NY, to_y, lambda p: y2.at[y], y2.at[y], lambda p: y2.at[y_of(p)])

    with jax.named_scope("gather_over_plane"):
        for wait in earlier:
            wait()

        def forward(p):
            q = (here + NP - p) % NP
            there = full.at[c, q // NY, q % NY]
            copy("plane", p, out_block, there, to_plane(p)).wait_recv()
            copy("core", q, there, there, to_core).start()

        each(NP, forward)
        departures.append(lambda: each(NP, lambda q: copy("core", q, out_block, out_block, to_core).wait_send(), 0))

    with jax.named_scope("layer_grads_over_rep"):
        arrive("y2")
        g1_out[...] = jnp.sum(y2[...], axis=0)

    with jax.named_scope("gather_over_core"):
        def from_core(q):
            there = full.at[1 - c, q // NY, q % NY]
            copy("core", q, there, there, to_core).wait_recv()

        each(NP, from_core, 0)

    with jax.named_scope("sends"):
        depart()


def finish_kernel(full, g1, *refs):
    outs, bufs, sem = refs[0:7], refs[7:14], refs[14]
    loss, g1s, g1n, gb1, g2s, g2n, gb2 = bufs
    for d in range(NG):
        cut = slice(d * SPAN, (d + 1) * SPAN)
        g1s[:, cut] = g1[d, 0:COLS]
        g1n[:, cut] = g1[d, COLS:2 * COLS]
        gb1[d:d + 1, :] = g1[d, 2 * COLS:2 * COLS + 1]
    rows = full[0, 0, NY - 1].astype(f32)
    at = TAIL_AT - (NY - 1) * PART
    tail = rows[at:at + 2] + rows[at + 2:at + 4]
    gb2[:, 0:SPAN] = tail[0:1]
    gb2[:, SPAN:CLASSES] = tail[1:2, 0:CLASSES - SPAN]
    loss[...] = tail[1:2, LOSS_LANE - SPAN:LOSS_LANE - SPAN + 1] / TARGETS
    stores = []

    def store(src, dst):
        stores.append(pltpu.make_async_copy(src, dst, sem.at[len(stores)]))
        stores[-1].start()

    for i in (0, 1, 2, 3, 6):
        store(bufs[i], outs[i])
    for d in range(NG):
        cut = slice(d * SPAN, (d + 1) * SPAN)
        flat = full[d % 2, d // 2].astype(f32).reshape(GRAD_ROWS, SPAN)
        g2s[:, cut] = flat[0:CLASSES]
        g2n[:, cut] = flat[NBR_AT:NBR_AT + CLASSES]
        store(g2s.at[:, cut], outs[4].at[:, cut])
        store(g2n.at[:, cut], outs[5].at[:, cut])
    for copied in stores:
        copied.wait()


def per_device(
    features, self_ids, nbr_ids, nbr_counts, w1_self, w1_nbr, bias1, w2_self, w2_nbr, bias2, labels, top_ids, top_counts
):
    hidden = bias1.shape[0]
    operands = (
        features.T, self_ids.T, jnp.transpose(nbr_ids, (2, 1, 0)), nbr_counts.T, w1_self, w1_nbr,
        bias1.reshape(NG, SPAN), w2_self.T, w2_nbr.T, bias2.reshape(1, CLASSES), labels.reshape(1, 8),
        top_ids, top_counts.reshape(1, 8),
    )
    scratch = [VMEM(a.shape, a.dtype) for a in operands] + [
        VMEM((LOW // SPAN, HIGH * 8, SPAN), f32),
        VMEM((HIGH * COLS, LOW), bf16),
        VMEM((16, hidden), f32),
        VMEM((NG, 16, SPAN), bf16),
        VMEM((NG, 16, SPAN), bf16),
        VMEM((4, 4, SPAN, SPAN), bf16),
        VMEM((NG, 8, SPAN), f32),
        VMEM((8, SPAN, SPAN), f32),
        VMEM((8 * SPAN, SPAN), f32),
        VMEM((8, 16, SPAN), bf16),
        VMEM((NZ, 16, SPAN), bf16),
        VMEM((NZ, 16, SPAN), bf16),
        VMEM((8, 16, SPAN), bf16),
        VMEM((NG, 8, 16, SPAN), bf16),
        VMEM((NG, 8, 16, SPAN), bf16),
        VMEM((NG, 8, 2 * SPAN), f32),
        VMEM((NG, 8, 2 * SPAN), f32),
        VMEM((8, 2 * SPAN), f32),
        VMEM((NG, 8, 2 * SPAN), f32),
        VMEM((4, 4, 64, SPAN), bf16),
        VMEM((GRAD_ROWS, SPAN), f32),
        VMEM((4, NY, BLOCK, SPAN), f32),
        VMEM((4, BLOCK, SPAN), f32),
        VMEM((4, BLOCK, SPAN), f32),
        VMEM((NG, 16, SPAN), f32),
        VMEM((NG, 16, SPAN), f32),
        VMEM((NY, NG, 16, SPAN), f32),
        pltpu.SemaphoreType.DMA((total_sems,)),
        pltpu.SemaphoreType.DMA((total_sems,)),
        pltpu.SemaphoreType.DMA((len(operands),)),
    ]
    full, g1 = pl.pallas_call(
        step_kernel,
        out_shape=[
            jax.ShapeDtypeStruct((2, NX, NY, PART, SPAN), bf16), jax.ShapeDtypeStruct((NG, 16, SPAN), f32),
        ],
        in_specs=[pl.BlockSpec(memory_space=pltpu.HBM)] * len(operands),
        out_specs=[pl.BlockSpec(memory_space=VMEM)] * 2,
        scratch_shapes=scratch,
        compiler_params=pltpu.CompilerParams(
            collective_id=0, has_side_effects=True, vmem_limit_bytes=60 * 2**20
        ),
        name="step",
    )(*operands)
    shapes = (
        (1, 1), (COLS, hidden), (COLS, hidden), (NG, SPAN), (CLASSES, hidden), (CLASSES, hidden), (1, CLASSES),
    )
    loss, g1s, g1n, gb1, g2s, g2n, gb2 = pl.pallas_call(
        finish_kernel,
        out_shape=[jax.ShapeDtypeStruct(s, f32) for s in shapes],
        in_specs=[pl.BlockSpec(memory_space=VMEM)] * 2,
        out_specs=[pl.BlockSpec(memory_space=pltpu.HBM)] * len(shapes),
        scratch_shapes=[VMEM(s, f32) for s in shapes] + [pltpu.SemaphoreType.DMA((5 + 2 * NG,))],
        name="finish",
    )(full, g1)
    return loss.reshape(()), g1s, g1n, gb1.reshape(hidden), g2s.T, g2n.T, gb2.reshape(CLASSES)


def solution(mesh):
    in_specs = (
        P(None, "cols"), P(None, "rep"), P(None, "rep", None), P(None, "rep"), P("cols", None), P("cols", None),
        P(), P(), P(), P(), P(("cols", "rep")), P(("cols", "rep"), None), P(("cols", "rep")),
    )
    out_specs = (P(), P("cols", None), P("cols", None), P(), P(), P(), P())
    return jax.shard_map(per_device, mesh=mesh, in_specs=in_specs, out_specs=out_specs, check_vma=False)
```

```python
import jax
import jax.numpy as jnp
from jax import lax
from jax.experimental import pallas as pl
from jax.experimental.pallas import tpu as pltpu
from jax.sharding import PartitionSpec as P

f32, bf16 = jnp.float32, jnp.bfloat16
loss_scale = 64.0

NZ, NG, NY, NX = 16, 8, 4, 4
TARGETS = 8 * NZ * NG * NY
LOW = 512
HIGH = 65536 // LOW
COLS = 6
FAN = 25
CLASSES = 153
LOSS_LANE = 200
SPAN = 128
NP = NX * NY
NBR_AT = 159
TAIL_AT = 312
GRAD_ROWS = 384
PART = GRAD_ROWS // NY
BLOCK = PART // 4
NEAR = (0, 1, NZ - 1, 2)
VMEM = pltpu.VMEM

SEMS = {}
total_sems = 0
for stage, slots in (
    ("w_g", NG), ("aux", NG), ("w_far", 4), ("w_near", 4), ("x_z", NZ), ("x_g", NG), ("xg", NG), ("lr", NG), ("gl", NG),
    ("gp_far", 4), ("gp_near", 4), ("scatter", 16), ("far", 4), ("near", 4), ("plane", NP), ("core", NP),
    ("dw", NG), ("y2", NY),
):
    SEMS[stage] = total_sems
    total_sems += slots


def dot(a, b, ca=1, cb=0):
    return lax.dot_general(a, b, (((ca,), (cb,)), ((), ())), preferred_element_type=f32)


def iota(shape, dim):
    return lax.broadcasted_iota(jnp.int32, shape, dim)


def step_kernel(
    feat_hbm, self_hbm, nbr_hbm, counts_hbm, w1s_hbm, w1n_hbm, bias1_hbm, w2s_hbm, w2n_hbm, bias2_hbm, labels_hbm,
    top_hbm, top_counts_hbm, full, g1_out,
    feat, self_ids, nbr_ids, nbr_counts, w1s, w1n, bias1, w2s, w2n, bias2, labels, top_ids, top_counts,
    split, table, wt, w_src, w_mid, w_all, aux, rows_t, rows_m, xp, x_src, x_in, x_mid, x_all, xg,
    lp, lr, gl_src, gl_all, gp_all, g2, ra, rb, rc, spread, dw_src, dw_in, y2, send_sem, recv_sem, load_sem, keep_sem,
):
    o = lax.axis_index("cols")
    y = lax.axis_index("rep")
    z = o // NG
    g = o % NG
    x = g // 2
    c = g % 2
    here = x * NY + y

    def to_z(p):
        return {"cols": ((z + p) % NZ) * NG + g, "rep": y}

    def to_g(p):
        return {"cols": z * NG + (g + p) % NG, "rep": y}

    def to_y(p):
        return {"cols": o, "rep": (y + p) % NY}

    def to_plane(p):
        q = (here + p) % NP
        return {"cols": z * NG + (q // NY) * 2 + c, "rep": q % NY}

    to_core = {"cols": z * NG + x * 2 + (1 - c), "rep": y}

    def copy(stage, p, src, dst, device):
        at = SEMS[stage] + p
        return pltpu.make_async_remote_copy(
            src_ref=src, dst_ref=dst, send_sem=send_sem.at[at], recv_sem=recv_sem.at[at], device_id=device
        )

    def each(n, body, first=1):
        def run(p, carry):
            body(p)
            return carry
        lax.fori_loop(first, n, run, 0)

    arrivals, departures = {}, []

    def launch(stage, n, device, src, dst, got):
        def begin(i):
            p = n // 2 + ((i + 1) // 2) * (2 * (i % 2) - 1)
            copy(stage, p, src(p), dst, device(p)).start()

        each(n - 1, begin, 0)
        arrivals[stage] = lambda: each(n, lambda p: copy(stage, p, src(p), got(p), device(p)).wait_recv())
        departures.append(lambda: each(n, lambda p: copy(stage, p, src(p), dst, device(p)).wait_send()))

    def launch_near(stage, src, dst, got):
        steps = list(enumerate(NEAR))[1:]
        for i, p in steps:
            copy(stage, i, src, dst, to_z(p)).start()

        def wait_near():
            for i, p in steps:
                copy(stage, i, src, got((z + NZ - p) % 4), to_z(p)).wait_recv()

        def sent_near():
            for i, p in steps:
                copy(stage, i, src, dst, to_z(p)).wait_send()

        arrivals[stage] = wait_near
        departures.append(sent_near)

    def arrive(stage):
        arrivals.pop(stage)()

    def depart():
        while departures:
            departures.pop(0)()

    def to_far(p):
        return to_z(4 * p)

    row, col = z % 4, z // 4

    def far_of(p):
        return (col + 4 - p) % 4

    def z_of(p):
        return (z + NZ - p) % NZ

    def g_of(p):
        return (g + NG - p) % NG

    def y_of(p):
        return (y + NY - p) % NY

    loads = [
        pltpu.make_async_copy(src, dst, load_sem.at[i])
        for i, (src, dst) in enumerate((
            (feat_hbm, feat), (w1s_hbm, w1s), (w1n_hbm, w1n), (top_counts_hbm, top_counts), (labels_hbm, labels),
            (top_hbm, top_ids), (self_hbm, self_ids), (counts_hbm, nbr_counts), (nbr_hbm, nbr_ids),
            (bias1_hbm, bias1), (bias2_hbm, bias2), (w2s_hbm, w2s), (w2n_hbm, w2n),
        ))
    ]
    for load in loads:
        load.start()
    waiting = list(range(13))

    def ready(first, last):
        for i in range(first, last):
            waiting.remove(i)
            loads[i].wait()

    barrier = pltpu.get_barrier_semaphore()
    others = [to_z(p) for p in sorted(range(1, NZ), key=lambda p: abs(p - NZ // 2))]
    others += [
        {"cols": ((z + step) % NZ) * NG + g, "rep": (y + p) % NY} for step in NEAR[1:] + (NZ - 2,) for p in range(1, NY)
    ]
    others += [{"cols": z * NG + i * 2 + c, "rep": (y + p) % NY} for i in range(NX) for p in range(1, NY)]
    others += [to_g(p) for p in range(1, NG)]
    n_others = len(others)

    def greet(n):
        for device in others[:n]:
            pl.semaphore_signal(barrier, inc=1, device_id=device)
        del others[:n]

    greet(NZ - 1)

    with jax.named_scope("prepare"):
        wt[...] = jnp.zeros_like(wt)
        ready(1, 6)
        wt[0:COLS, :] = w1s[...].astype(f32)
        wt[COLS:2 * COLS, :] = w1n[...].astype(f32)
        for d in range(NG):
            w_src[d] = wt[:, d * SPAN:(d + 1) * SPAN].astype(bf16)
        w_mid[g] = w_src[g]

        eye = iota((8, 8), 0) == iota((8, 8), 1)

        def column(ref):
            return jnp.sum(jnp.where(eye, jnp.broadcast_to(ref[...].astype(f32), (8, 8)), 0.0), axis=1, keepdims=True)

        count_col = column(top_counts)
        label_col = column(labels)
        picks = top_ids[...]
        live_top = iota(picks.shape, 1).astype(f32) < count_col
        lane = iota((8, SPAN), 1)
        mine = jnp.where(lane == 8, count_col, jnp.where(lane == 9, label_col, 0.0))
        for s in range(8):
            n_s = jnp.sum(jnp.where(live_top & (picks == s), 1.0, 0.0), axis=1, keepdims=True)
            mine = jnp.where(lane == s, n_s, mine)
        aux[g] = mine

    with jax.named_scope("table"):
        ready(0, 1)

        for h in range(HIGH):
            piece = feat[:, h * LOW:(h + 1) * LOW].astype(f32)
            for q in range(LOW // SPAN):
                split[q, h * 8:h * 8 + COLS, :] = piece[:, q * SPAN:(q + 1) * SPAN]
            if h % 3 == 2:
                greet(1)
        greet(len(others))
        for k in range(COLS):
            for q in range(LOW // SPAN):
                table[k * HIGH:(k + 1) * HIGH, q * SPAN:(q + 1) * SPAN] = (
                    split[q, pl.ds(k, HIGH, stride=8), :].astype(bf16)
                )

    with jax.named_scope("lookup"):
        ready(6, 9)
        io_low = iota((256, SPAN), 0).astype(f32).astype(bf16)
        io_high = iota((HIGH, SPAN), 0)
        counts = nbr_counts[...]

        def look(ids, alive):
            low = jnp.bitwise_and(ids, LOW - 1).astype(f32)
            high = jnp.where(alive, jnp.right_shift(ids, LOW.bit_length() - 1), -1)

            def hot_rows(first, j):
                at = jnp.broadcast_to((low[j:j + 1, :] - first).astype(bf16), (256, SPAN))
                return jnp.where(io_low == at, jnp.bfloat16(1), jnp.bfloat16(0))

            hot = jnp.concatenate([
                jnp.concatenate([hot_rows(float(first), j) for j in range(8)], axis=1) for first in range(0, LOW, 256)
            ], axis=0)
            mask = jnp.concatenate([io_high == high[j:j + 1, :] for j in range(8)], axis=1)
            got = dot(table[...], hot)
            return tuple(
                jnp.sum(jnp.where(mask, got[k * HIGH:(k + 1) * HIGH], 0.0).reshape(HIGH // 8, 8, 8 * SPAN), axis=0)
                for k in range(COLS)
            )

        def add_nbr(k, sums):
            return tuple(a + b for a, b in zip(sums, look(nbr_ids[k], counts > k)))

        own = look(self_ids[...], counts > 0)
        pl.semaphore_wait(barrier, n_others)
        launch("w_g", NG, to_g, lambda p: w_src.at[(g + p) % NG], w_mid.at[g], lambda p: w_mid.at[g_of(p)])
        launch("aux", NG, to_g, lambda p: aux.at[g], aux.at[g], lambda p: aux.at[g_of(p)])
        sums = tuple(jnp.zeros((8, 8 * SPAN), f32) for _ in range(COLS))
        sums = lax.fori_loop(0, 5, add_nbr, sums, unroll=5)
        arrive("w_g")
        w_all[row, col] = w_mid[...].reshape(SPAN, SPAN)
        w_mine = w_all.at[row, col]
        launch("w_far", 4, to_far, lambda p: w_mine, w_mine, lambda p: w_all.at[row, far_of(p)])
        sums = lax.fori_loop(5, 15, add_nbr, sums, unroll=5)
        arrive("w_far")
        launch_near("w_near", w_all.at[row], w_all.at[row], lambda r: w_all.at[r])
        sums = lax.fori_loop(15, FAN, add_nbr, sums, unroll=5)

    with jax.named_scope("rows"):
        rows_t[...] = jnp.zeros_like(rows_t)
        for j in range(8):
            cut = slice(j * SPAN, (j + 1) * SPAN)
            count = counts[j:j + 1, :].astype(f32)
            for k in range(COLS):
                rows_t[j, k:k + 1, :] = jnp.sum(own[k][:, cut], axis=0, keepdims=True)
                rows_t[j, COLS + k:COLS + k + 1, :] = jnp.sum(sums[k][:, cut], axis=0, keepdims=True) / count
            rows_t[j, 2 * COLS:2 * COLS + 1, :] = jnp.ones((1, SPAN), f32)
        for j in range(8):
            rows_m[pl.ds(j, SPAN, stride=8), :] = rows_t[j].T
        for t in range(8):
            xp[t] = rows_m[t * SPAN:(t + 1) * SPAN, :].T[0:16, :].astype(bf16)

        odd = z % 2
        half = iota((16, SPAN), 1) // 64
        for t in range(8):
            straight = xp[t].astype(f32)
            turned = pltpu.roll(straight, 64, 1)
            x_src[2 * t] = jnp.where(half == odd, jnp.where(odd == 0, straight, turned), 0.0).astype(bf16)
            x_src[2 * t + 1] = jnp.where(half == odd, jnp.where(odd == 1, straight, turned), 0.0).astype(bf16)
        launch("x_z", NZ, to_z, lambda p: x_src.at[(z + p) % NZ], x_in.at[z], lambda p: x_in.at[z_of(p)])
        x_in[z] = x_src[z]
        xg[g] = xp[...]

    with jax.named_scope("lists"):
        arrive("aux")
        lists = aux[...].reshape(64, SPAN)
        top_div = lists[:, 8:9]
        repeat = (iota((SPAN, 64), 0) == iota((SPAN, 64), 1) % 8).astype(f32).astype(bf16)
        same = iota((64, 64), 0) // 8 == iota((64, 64), 1) // 8
        picked = jnp.where(same, dot(lists.astype(bf16), repeat), 0.0).astype(bf16)
        ready(9, 13)

    with jax.named_scope("rows_to_z"):
        arrive("w_near")
        depart()
        arrive("x_z")
    for t in range(8):
        x_mid[t] = x_in[2 * t] + x_in[2 * t + 1]
    launch("x_g", NG, to_g, lambda p: x_mid, x_all.at[g], lambda p: x_all.at[g_of(p)])
    x_all[g] = x_mid[...]

    with jax.named_scope("rows_over_g"):
        arrive("x_g")

    with jax.named_scope("layers"):
        both = jnp.zeros((SPAN, 2 * SPAN), f32)
        for t in range(8):
            left = x_all[:, t].reshape(SPAN, SPAN)
            right = jnp.concatenate([w_all[(2 * t + i) % 4, (2 * t + i) // 4] for i in range(2)], axis=1)
            both = both + dot(left, right, 0, 0)
        pre = both[0:64, 0:SPAN] + both[64:SPAN, SPAN:] + bias1[pl.ds(g, 1), :]
        hidden = jnp.maximum(pre, 0.0).astype(bf16)
        top_mean = (dot(picked, hidden) / top_div).astype(bf16)
        span = pl.ds(pl.multiple_of(g * SPAN, SPAN), SPAN)
        w2s_g = w2s[:, span]
        w2n_g = w2n[:, span]
        part = dot(hidden, w2s_g, 1, 1) + dot(top_mean, w2n_g, 1, 1)
        lp[...] = jnp.zeros_like(lp)
        lp[:, :, 0:CLASSES] = part.reshape(NG, 8, CLASSES)
        launch("lr", NG, to_g, lambda p: lp.at[(g + p) % NG], lr.at[g], lambda p: lr.at[g_of(p)])
        lr[g] = lp[g]
    with jax.named_scope("logits_wait"):
        depart()
        arrive("lr")

    with jax.named_scope("softmax"):
        logits = jnp.sum(lr[...], axis=0)[:, 0:CLASSES] + bias2[...]
        exps = jnp.exp(logits)
        total = jnp.sum(exps, axis=1, keepdims=True)
        onehot = jnp.where(iota((8, CLASSES), 1).astype(f32) == label_col, 1.0, 0.0)
        row_loss = jnp.log(total) - jnp.sum(onehot * logits, axis=1, keepdims=True)
        grad = ((exps / total - onehot) * (loss_scale / TARGETS)).astype(bf16)
        gl_src[...] = jnp.where(iota((8, 2 * SPAN), 1) == LOSS_LANE, row_loss, 0.0)
        gl_src[:, 0:CLASSES] = grad.astype(f32)
        launch("gl", NG, to_g, lambda p: gl_src, gl_all.at[g], lambda p: gl_all.at[g_of(p)])
        gl_all[g] = gl_src[...]
        g2[...] = jnp.zeros_like(g2)
    with jax.named_scope("grad_logits_wait"):
        arrive("gl")

    with jax.named_scope("classifier_grads"):
        gl_rows = gl_all[...].reshape(64, 2 * SPAN)
        gl = gl_rows[:, 0:CLASSES].astype(bf16)
        g2[0:CLASSES, :] = dot(gl, hidden, 0, 0)
        g2[NBR_AT:NBR_AT + CLASSES, :] = dot(gl, top_mean, 0, 0)
        col_sums = jnp.sum(gl_rows, axis=0, keepdims=True)
        g2[TAIL_AT:TAIL_AT + 1, :] = col_sums[:, 0:SPAN]
        g2[TAIL_AT + 1:TAIL_AT + 2, :] = col_sums[:, SPAN:]

        def block(r, d):
            return g2.at[pl.ds(pl.multiple_of((d * 4 + r) * BLOCK, 8), BLOCK)]

        def scatter(act, wait=False):
            for i, p in enumerate(NEAR):
                def run(q, i=i, p=p):
                    device = {"cols": ((z + p) % NZ) * NG + g, "rep": (y + q) % NY}
                    got = ra.at[i, y_of(q)] if wait else ra.at[i, y]
                    act(copy("scatter", i * 4 + q, block((z + p) % 4, (y + q) % NY), got, device))

                each(NY, run, 0 if i else 1)

        scatter(lambda send: send.start())
        departures.append(lambda: scatter(lambda send: send.wait_send()))
        ra[0, y] = g2[pl.ds(pl.multiple_of((y * 4 + row) * BLOCK, 8), BLOCK), :]

    with jax.named_scope("back"):
        back_top = dot(gl, w2n_g) / top_div
        top_1 = back_top.astype(bf16)
        rest = back_top - top_1.astype(f32)
        top_2 = rest.astype(bf16)
        top_3 = (rest - top_2.astype(f32)).astype(bf16)
        back = dot(gl, w2s_g) + (dot(picked, top_1, 0, 0) + (dot(picked, top_2, 0, 0) + dot(picked, top_3, 0, 0)))
        grad_pre = jnp.where(pre > 0.0, back, 0.0).astype(bf16)
        gp_all[row, col] = grad_pre
        mine_gp = gp_all.at[row, col]
        launch("gp_far", 4, to_far, lambda p: mine_gp, mine_gp, lambda p: gp_all.at[row, far_of(p)])
        launch("xg", NG, to_g, lambda p: xp, xg.at[g], lambda p: xg.at[g_of(p)])

    with jax.named_scope("scatter"):
        scatter(lambda send: send.wait_recv(), wait=True)
        rb[col] = jnp.sum(ra[...].reshape(4 * NY, BLOCK, SPAN), axis=0)
        mine_rb = rb.at[col]
        launch("far", 4, to_far, lambda p: mine_rb, mine_rb, lambda p: rb.at[far_of(p)])

    with jax.named_scope("grad_pre_far"):
        arrive("gp_far")
        launch_near("gp_near", gp_all.at[row], gp_all.at[row], lambda r: gp_all.at[r])

    with jax.named_scope("far"):
        arrive("far")
        rc[row] = jnp.sum(rb[...], axis=0)
        launch_near("near", rc.at[row], rc.at[row], lambda r: rc.at[r])

    with jax.named_scope("grad_pre_near"):
        arrive("xg")
        arrive("gp_near")
    with jax.named_scope("layer_grads"):
        dw = jnp.zeros((SPAN, SPAN), f32)
        for t in range(8):
            pair = [gp_all[(2 * t + i) % 4, (2 * t + i) // 4] for i in range(2)]
            dw = dw + dot(xg[:, t].reshape(SPAN, SPAN), jnp.concatenate(pair, axis=0))
        dw_src[...] = dw.reshape(NG, 16, SPAN)
        launch("dw", NG, to_g, lambda p: dw_src.at[(g + p) % NG], dw_in.at[g], lambda p: dw_in.at[g_of(p)])
        dw_in[g] = dw_src[g]

    with jax.named_scope("gather_over_z"):
        arrive("near")
        earlier = departures[:]
        departures.clear()
        fin = rc[...].reshape(PART, SPAN)
        low_part = fin - fin.astype(bf16).astype(f32)
        low_part = jnp.concatenate([low_part[0:2], low_part[0:PART - 2]], axis=0)
        at = iota((PART, SPAN), 0) - (TAIL_AT - (NY - 1) * PART)
        is_low = (y == NY - 1) & (at >= 2) & (at < 4)
        spread[x, y] = jnp.where(is_low, low_part, fin).astype(bf16)
        out_block = spread.at[x, y]
        each(NP, lambda p: copy("plane", p, out_block, out_block, to_plane(p)).start())

        def keep(q):
            return pltpu.make_async_copy(spread.at[q // NY, q % NY], full.at[c, q // NY, q % NY], keep_sem.at[q])

        def to_other_core(q):
            return copy("core", q, spread.at[q // NY, q % NY], full.at[c, q // NY, q % NY], to_core)

        keep(here).start()
        to_other_core(here).start()

    with jax.named_scope("layer_grads_wait"):
        arrive("dw")
        y2[y] = dw_in[...].astype(bf16)
        launch("y2", NY, to_y, lambda p: y2.at[y], y2.at[y], lambda p: y2.at[y_of(p)])

    with jax.named_scope("gather_over_plane"):
        for wait in earlier:
            wait()

        def forward(p):
            q = (here + NP - p) % NP
            copy("plane", p, out_block, spread.at[q // NY, q % NY], to_plane(p)).wait_recv()
            to_other_core(q).start()
            keep(q).start()

        each(NP, forward)
        departures.append(lambda: each(NP, lambda p: copy("plane", p, out_block, out_block, to_plane(p)).wait_send()))
        departures.append(lambda: each(NP, lambda q: to_other_core(q).wait_send(), 0))
        departures.append(lambda: each(NP, lambda q: keep(q).wait(), 0))

    with jax.named_scope("layer_grads_over_rep"):
        arrive("y2")
        g1_out[...] = jnp.sum(y2[...].astype(f32), axis=0)

    with jax.named_scope("gather_over_core"):
        def from_core(q):
            copy("core", q, spread.at[q // NY, q % NY], full.at[1 - c, q // NY, q % NY], to_core).wait_recv()

        each(NP, from_core, 0)

    with jax.named_scope("sends"):
        depart()


def finish_kernel(full_hbm, g1_hbm, *refs):
    outs, bufs, full, g1, load_sem, sem = refs[0:7], refs[7:14], refs[14], refs[15], refs[16], refs[17]
    loss, g1s, g1n, gb1, g2s, g2n, gb2 = bufs
    blocks = [
        pltpu.make_async_copy(full_hbm.at[d % 2, d // 2], full.at[d % 2, d // 2], load_sem.at[d]) for d in range(NG)
    ]
    small = pltpu.make_async_copy(g1_hbm, g1, load_sem.at[NG])
    small.start()
    for block in blocks:
        block.start()
    small.wait()
    for d in range(NG):
        cut = slice(d * SPAN, (d + 1) * SPAN)
        g1s[:, cut] = g1[d, 0:COLS]
        g1n[:, cut] = g1[d, COLS:2 * COLS]
        gb1[d:d + 1, :] = g1[d, 2 * COLS:2 * COLS + 1]
    blocks[0].wait()
    rows = full[0, 0, NY - 1].astype(f32)
    at = TAIL_AT - (NY - 1) * PART
    tail = rows[at:at + 2] + rows[at + 2:at + 4]
    gb2[:, 0:SPAN] = tail[0:1]
    gb2[:, SPAN:CLASSES] = tail[1:2, 0:CLASSES - SPAN]
    loss[...] = tail[1:2, LOSS_LANE - SPAN:LOSS_LANE - SPAN + 1] / TARGETS
    stores = []

    def store(src, dst):
        stores.append(pltpu.make_async_copy(src, dst, sem.at[len(stores)]))
        stores[-1].start()

    for i in (0, 1, 2, 3, 6):
        store(bufs[i], outs[i])
    for d in range(NG):
        cut = slice(d * SPAN, (d + 1) * SPAN)
        if d:
            blocks[d].wait()
        flat = full[d % 2, d // 2].astype(f32).reshape(GRAD_ROWS, SPAN)
        g2s[:, cut] = flat[0:CLASSES]
        g2n[:, cut] = flat[NBR_AT:NBR_AT + CLASSES]
        store(g2s.at[:, cut], outs[4].at[:, cut])
        store(g2n.at[:, cut], outs[5].at[:, cut])
    for copied in stores:
        copied.wait()


def per_device(
    features, self_ids, nbr_ids, nbr_counts, w1_self, w1_nbr, bias1, w2_self, w2_nbr, bias2, labels, top_ids, top_counts
):
    hidden = bias1.shape[0]
    operands = (
        features.T, self_ids.T, jnp.transpose(nbr_ids, (2, 1, 0)), nbr_counts.T, w1_self, w1_nbr,
        bias1.reshape(NG, SPAN), w2_self.T, w2_nbr.T, bias2.reshape(1, CLASSES), labels.reshape(1, 8),
        top_ids, top_counts.reshape(1, 8),
    )
    scratch = [VMEM(a.shape, a.dtype) for a in operands] + [
        VMEM((LOW // SPAN, HIGH * 8, SPAN), f32),
        VMEM((HIGH * COLS, LOW), bf16),
        VMEM((16, hidden), f32),
        VMEM((NG, 16, SPAN), bf16),
        VMEM((NG, 16, SPAN), bf16),
        VMEM((4, 4, SPAN, SPAN), bf16),
        VMEM((NG, 8, SPAN), f32),
        VMEM((8, SPAN, SPAN), f32),
        VMEM((8 * SPAN, SPAN), f32),
        VMEM((8, 16, SPAN), bf16),
        VMEM((NZ, 16, SPAN), bf16),
        VMEM((NZ, 16, SPAN), bf16),
        VMEM((8, 16, SPAN), bf16),
        VMEM((NG, 8, 16, SPAN), bf16),
        VMEM((NG, 8, 16, SPAN), bf16),
        VMEM((NG, 8, 2 * SPAN), f32),
        VMEM((NG, 8, 2 * SPAN), f32),
        VMEM((8, 2 * SPAN), f32),
        VMEM((NG, 8, 2 * SPAN), f32),
        VMEM((4, 4, 64, SPAN), bf16),
        VMEM((GRAD_ROWS, SPAN), f32),
        VMEM((4, NY, BLOCK, SPAN), f32),
        VMEM((4, BLOCK, SPAN), f32),
        VMEM((4, BLOCK, SPAN), f32),
        VMEM((NX, NY, PART, SPAN), bf16),
        VMEM((NG, 16, SPAN), f32),
        VMEM((NG, 16, SPAN), f32),
        VMEM((NY, NG, 16, SPAN), bf16),
        pltpu.SemaphoreType.DMA((total_sems,)),
        pltpu.SemaphoreType.DMA((total_sems,)),
        pltpu.SemaphoreType.DMA((len(operands),)),
        pltpu.SemaphoreType.DMA((NP,)),
    ]
    full, g1 = pl.pallas_call(
        step_kernel,
        out_shape=[
            jax.ShapeDtypeStruct((2, NX, NY, PART, SPAN), bf16), jax.ShapeDtypeStruct((NG, 16, SPAN), f32),
        ],
        in_specs=[pl.BlockSpec(memory_space=pltpu.HBM)] * len(operands),
        out_specs=[pl.BlockSpec(memory_space=pltpu.HBM), pl.BlockSpec(memory_space=VMEM)],
        scratch_shapes=scratch,
        compiler_params=pltpu.CompilerParams(
            collective_id=0, has_side_effects=True, vmem_limit_bytes=60 * 2**20
        ),
        name="step",
    )(*operands)
    shapes = (
        (1, 1), (COLS, hidden), (COLS, hidden), (NG, SPAN), (CLASSES, hidden), (CLASSES, hidden), (1, CLASSES),
    )
    loss, g1s, g1n, gb1, g2s, g2n, gb2 = pl.pallas_call(
        finish_kernel,
        out_shape=[jax.ShapeDtypeStruct(s, f32) for s in shapes],
        in_specs=[pl.BlockSpec(memory_space=pltpu.HBM)] * 2,
        out_specs=[pl.BlockSpec(memory_space=pltpu.HBM)] * len(shapes),
        scratch_shapes=[VMEM(s, f32) for s in shapes] + [
            VMEM(full.shape, bf16), VMEM(g1.shape, f32),
            pltpu.SemaphoreType.DMA((NG + 1,)), pltpu.SemaphoreType.DMA((5 + 2 * NG,)),
        ],
        compiler_params=pltpu.CompilerParams(vmem_limit_bytes=60 * 2**20),
        name="finish",
    )(full, g1)
    return loss.reshape(()), g1s, g1n, gb1.reshape(hidden), g2s.T, g2n.T, gb2.reshape(CLASSES)


def solution(mesh):
    in_specs = (
        P(None, "cols"), P(None, "rep"), P(None, "rep", None), P(None, "rep"), P("cols", None), P("cols", None),
        P(), P(), P(), P(), P(("cols", "rep")), P(("cols", "rep"), None), P(("cols", "rep")),
    )
    out_specs = (P(), P("cols", None), P("cols", None), P(), P(), P(), P())
    return jax.shard_map(per_device, mesh=mesh, in_specs=in_specs, out_specs=out_specs, check_vma=False)
```

```python
import jax
import jax.numpy as jnp
from jax import lax
from jax.experimental import pallas as pl
from jax.experimental.pallas import tpu as pltpu
from jax.sharding import PartitionSpec as P

f32, bf16 = jnp.float32, jnp.bfloat16
loss_scale = 64.0

NZ, NG, NY, NX = 16, 8, 4, 4
TARGETS = 8 * NZ * NG * NY
LOW = 512
HIGH = 65536 // LOW
COLS = 6
FAN = 25
CLASSES = 153
LOSS_LANE = 200
SPAN = 128
NP = NX * NY
NBR_AT = 159
TAIL_AT = 312
GRAD_ROWS = 384
PART = GRAD_ROWS // NY
BLOCK = PART // 4
NEAR = (0, 1, NZ - 1, 2)
VMEM = pltpu.VMEM

SEMS = {}
total_sems = 0
for stage, slots in (
    ("w_g", NG), ("aux", NG), ("w_far", 4), ("w_near", 4), ("x_z", NZ), ("x_g0", NG), ("x_g1", NG), ("xg", NG), ("lr", NG), ("gl", NG),
    ("gp_far", 4), ("gp_near", 4), ("scatter", 16), ("far", 4), ("near", 4), ("plane", NP), ("core", NP),
    ("dw", NG), ("y2", NY),
):
    SEMS[stage] = total_sems
    total_sems += slots


def dot(a, b, ca=1, cb=0):
    return lax.dot_general(a, b, (((ca,), (cb,)), ((), ())), preferred_element_type=f32)


def iota(shape, dim):
    return lax.broadcasted_iota(jnp.int32, shape, dim)


def step_kernel(
    feat_hbm, self_hbm, nbr_hbm, counts_hbm, w1s_hbm, w1n_hbm, bias1_hbm, w2s_hbm, w2n_hbm, bias2_hbm, labels_hbm,
    top_hbm, top_counts_hbm, full, g1_out,
    feat, self_ids, nbr_ids, nbr_counts, w1s, w1n, bias1, w2s, w2n, bias2, labels, top_ids, top_counts,
    split, table, wt, w_src, w_mid, w_all, aux, rows_t, rows_m, xp, x_src, x_in, x_mid, x_all, xg,
    lp, lr, gl_src, gl_all, gp_all, g2, ra, rb, rc, spread, dw_src, dw_in, y2, send_sem, recv_sem, load_sem, keep_sem,
):
    o = lax.axis_index("cols")
    y = lax.axis_index("rep")
    z = o // NG
    g = o % NG
    x = g // 2
    c = g % 2
    here = x * NY + y

    def to_z(p):
        return {"cols": ((z + p) % NZ) * NG + g, "rep": y}

    def to_g(p):
        return {"cols": z * NG + (g + p) % NG, "rep": y}

    def to_y(p):
        return {"cols": o, "rep": (y + p) % NY}

    def to_plane(p):
        q = (here + p) % NP
        return {"cols": z * NG + (q // NY) * 2 + c, "rep": q % NY}

    to_core = {"cols": z * NG + x * 2 + (1 - c), "rep": y}

    def copy(stage, p, src, dst, device):
        at = SEMS[stage] + p
        return pltpu.make_async_remote_copy(
            src_ref=src, dst_ref=dst, send_sem=send_sem.at[at], recv_sem=recv_sem.at[at], device_id=device
        )

    def each(n, body, first=1):
        def run(p, carry):
            body(p)
            return carry
        lax.fori_loop(first, n, run, 0)

    arrivals, departures = {}, []

    def launch(stage, n, device, src, dst, got):
        def begin(i):
            p = n // 2 + ((i + 1) // 2) * (2 * (i % 2) - 1)
            copy(stage, p, src(p), dst, device(p)).start()

        each(n - 1, begin, 0)
        arrivals[stage] = lambda: each(n, lambda p: copy(stage, p, src(p), got(p), device(p)).wait_recv())
        departures.append(lambda: each(n, lambda p: copy(stage, p, src(p), dst, device(p)).wait_send()))

    def launch_near(stage, src, dst, got):
        steps = list(enumerate(NEAR))[1:]
        for i, p in steps:
            copy(stage, i, src, dst, to_z(p)).start()

        def wait_near():
            for i, p in steps:
                copy(stage, i, src, got((z + NZ - p) % 4), to_z(p)).wait_recv()

        def sent_near():
            for i, p in steps:
                copy(stage, i, src, dst, to_z(p)).wait_send()

        arrivals[stage] = wait_near
        departures.append(sent_near)

    def arrive(stage):
        arrivals.pop(stage)()

    def depart():
        while departures:
            departures.pop(0)()

    def to_far(p):
        return to_z(4 * p)

    row, col = z % 4, z // 4

    def far_of(p):
        return (col + 4 - p) % 4

    def z_of(p):
        return (z + NZ - p) % NZ

    def g_of(p):
        return (g + NG - p) % NG

    def y_of(p):
        return (y + NY - p) % NY

    loads = [
        pltpu.make_async_copy(src, dst, load_sem.at[i])
        for i, (src, dst) in enumerate((
            (feat_hbm, feat), (w1s_hbm, w1s), (w1n_hbm, w1n), (top_counts_hbm, top_counts), (labels_hbm, labels),
            (top_hbm, top_ids), (self_hbm, self_ids), (counts_hbm, nbr_counts), (nbr_hbm, nbr_ids),
            (bias1_hbm, bias1), (bias2_hbm, bias2), (w2s_hbm, w2s), (w2n_hbm, w2n),
        ))
    ]
    for load in loads:
        load.start()
    waiting = list(range(13))

    def ready(first, last):
        for i in range(first, last):
            waiting.remove(i)
            loads[i].wait()

    barrier = pltpu.get_barrier_semaphore()
    others = [to_z(p) for p in sorted(range(1, NZ), key=lambda p: abs(p - NZ // 2))]
    others += [
        {"cols": ((z + step) % NZ) * NG + g, "rep": (y + p) % NY} for step in NEAR[1:] + (NZ - 2,) for p in range(1, NY)
    ]
    others += [{"cols": z * NG + i * 2 + c, "rep": (y + p) % NY} for i in range(NX) for p in range(1, NY)]
    others += [to_g(p) for p in range(1, NG)]
    n_others = len(others)

    def greet(n):
        for device in others[:n]:
            pl.semaphore_signal(barrier, inc=1, device_id=device)
        del others[:n]

    greet(NZ - 1)

    with jax.named_scope("prepare"):
        wt[...] = jnp.zeros_like(wt)
        ready(1, 6)
        wt[0:COLS, :] = w1s[...].astype(f32)
        wt[COLS:2 * COLS, :] = w1n[...].astype(f32)
        for d in range(NG):
            w_src[d] = wt[:, d * SPAN:(d + 1) * SPAN].astype(bf16)
        w_mid[g] = w_src[g]

        eye = iota((8, 8), 0) == iota((8, 8), 1)

        def column(ref):
            return jnp.sum(jnp.where(eye, jnp.broadcast_to(ref[...].astype(f32), (8, 8)), 0.0), axis=1, keepdims=True)

        count_col = column(top_counts)
        label_col = column(labels)
        picks = top_ids[...]
        live_top = iota(picks.shape, 1).astype(f32) < count_col
        lane = iota((8, SPAN), 1)
        mine = jnp.where(lane == 8, count_col, jnp.where(lane == 9, label_col, 0.0))
        for s in range(8):
            n_s = jnp.sum(jnp.where(live_top & (picks == s), 1.0, 0.0), axis=1, keepdims=True)
            mine = jnp.where(lane == s, n_s, mine)
        aux[g] = mine

    with jax.named_scope("table"):
        ready(0, 1)

        for h in range(HIGH):
            piece = feat[:, h * LOW:(h + 1) * LOW].astype(f32)
            for q in range(LOW // SPAN):
                split[q, h * 8:h * 8 + COLS, :] = piece[:, q * SPAN:(q + 1) * SPAN]
            if h % 3 == 2:
                greet(1)
        greet(len(others))
        for k in range(COLS):
            for q in range(LOW // SPAN):
                table[k * HIGH:(k + 1) * HIGH, q * SPAN:(q + 1) * SPAN] = (
                    split[q, pl.ds(k, HIGH, stride=8), :].astype(bf16)
                )

    with jax.named_scope("lookup"):
        ready(6, 9)
        io_low = iota((256, SPAN), 0).astype(f32).astype(bf16)
        io_high = iota((HIGH, SPAN), 0)
        counts = nbr_counts[...]

        def look(ids, alive):
            low = jnp.bitwise_and(ids, LOW - 1).astype(f32)
            high = jnp.where(alive, jnp.right_shift(ids, LOW.bit_length() - 1), -1)

            def hot_rows(first, j):
                at = jnp.broadcast_to((low[j:j + 1, :] - first).astype(bf16), (256, SPAN))
                return jnp.where(io_low == at, jnp.bfloat16(1), jnp.bfloat16(0))

            hot = jnp.concatenate([
                jnp.concatenate([hot_rows(float(first), j) for j in range(8)], axis=1) for first in range(0, LOW, 256)
            ], axis=0)
            mask = jnp.concatenate([io_high == high[j:j + 1, :] for j in range(8)], axis=1)
            got = dot(table[...], hot)
            found = []
            for k in range(COLS):
                one = jnp.zeros((8, 8 * SPAN), f32)
                for b in range(0, HIGH, 8):
                    one = jnp.where(mask[b:b + 8], got[k * HIGH + b:k * HIGH + b + 8], one)
                found.append(one)
            return tuple(found)

        def add_nbr(k, sums):
            return tuple(a + b for a, b in zip(sums, look(nbr_ids[k], counts > k)))

        own = look(self_ids[...], counts > 0)
        pl.semaphore_wait(barrier, n_others)
        launch("w_g", NG, to_g, lambda p: w_src.at[(g + p) % NG], w_mid.at[g], lambda p: w_mid.at[g_of(p)])
        launch("aux", NG, to_g, lambda p: aux.at[g], aux.at[g], lambda p: aux.at[g_of(p)])
        sums = tuple(jnp.zeros((8, 8 * SPAN), f32) for _ in range(COLS))
        sums = lax.fori_loop(0, 5, add_nbr, sums, unroll=5)
        arrive("w_g")
        w_all[row, col] = w_mid[...].reshape(SPAN, SPAN)
        w_mine = w_all.at[row, col]
        launch("w_far", 4, to_far, lambda p: w_mine, w_mine, lambda p: w_all.at[row, far_of(p)])
        sums = lax.fori_loop(5, 15, add_nbr, sums, unroll=5)
        arrive("w_far")
        launch_near("w_near", w_all.at[row], w_all.at[row], lambda r: w_all.at[r])
        sums = lax.fori_loop(15, FAN, add_nbr, sums, unroll=5)

    with jax.named_scope("rows"):
        rows_t[...] = jnp.zeros_like(rows_t)
        for j in range(8):
            cut = slice(j * SPAN, (j + 1) * SPAN)
            count = counts[j:j + 1, :].astype(f32)
            for k in range(COLS):
                rows_t[j, k:k + 1, :] = jnp.sum(own[k][:, cut], axis=0, keepdims=True)
                rows_t[j, COLS + k:COLS + k + 1, :] = jnp.sum(sums[k][:, cut], axis=0, keepdims=True) / count
            rows_t[j, 2 * COLS:2 * COLS + 1, :] = jnp.ones((1, SPAN), f32)
        for j in range(8):
            rows_m[pl.ds(j, SPAN, stride=8), :] = rows_t[j].T
        for t in range(8):
            xp[t] = rows_m[t * SPAN:(t + 1) * SPAN, :].T[0:16, :].astype(bf16)

        odd = z % 2
        half = iota((16, SPAN), 1) // 64
        for t in range(8):
            straight = xp[t].astype(f32)
            turned = pltpu.roll(straight, 64, 1)
            x_src[2 * t] = jnp.where(half == odd, jnp.where(odd == 0, straight, turned), 0.0).astype(bf16)
            x_src[2 * t + 1] = jnp.where(half == odd, jnp.where(odd == 1, straight, turned), 0.0).astype(bf16)
        launch("x_z", NZ, to_z, lambda p: x_src.at[(z + p) % NZ], x_in.at[z], lambda p: x_in.at[z_of(p)])
        x_in[z] = x_src[z]
        xg[g] = xp[...]

    with jax.named_scope("lists"):
        arrive("aux")
        lists = aux[...].reshape(64, SPAN)
        top_div = lists[:, 8:9]
        repeat = (iota((SPAN, 64), 0) == iota((SPAN, 64), 1) % 8).astype(f32).astype(bf16)
        same = iota((64, 64), 0) // 8 == iota((64, 64), 1) // 8
        picked = jnp.where(same, dot(lists.astype(bf16), repeat), 0.0).astype(bf16)
        ready(9, 13)
        lp[...] = jnp.zeros_like(lp)

    with jax.named_scope("rows_to_z"):
        arrive("w_near")
        arrivals.pop("x_z")
        pairs = [(z // 2 + p) % 8 for p in (0, 1, 7, 2, 6, 3, 5, 4)]

        def z_pair(i):
            for odd_z in range(2):
                if i == 0 and odd_z:
                    continue
                source = 2 * pairs[i] + odd_z if i else 2 * pairs[0] + 1 - odd
                copy("x_z", (z + NZ - source) % NZ, x_src.at[0], x_in.at[source], to_z(1)).wait_recv()
            x_mid[i // 4, i % 4] = x_in[2 * pairs[i]] + x_in[2 * pairs[i] + 1]

        for half_z in range(2):
            for i in range(4):
                z_pair(4 * half_z + i)
            launch(
                f"x_g{half_z}", NG, to_g, lambda p, h=half_z: x_mid.at[h], x_all.at[g, half_z],
                lambda p, h=half_z: x_all.at[g_of(p), h],
            )
        x_all[g] = x_mid[...]

    with jax.named_scope("rows_over_g"):
        depart()
        arrive("x_g0")
        arrive("x_g1")
    with jax.named_scope("layers"):
        both = jnp.zeros((SPAN, 2 * SPAN), f32)
        for t in range(8):
            left = x_all[:, t // 4, t % 4].reshape(SPAN, SPAN)
            sources = [2 * pairs[t] + i for i in range(2)]
            right = jnp.concatenate([w_all[source % 4, source // 4] for source in sources], axis=1)
            both = both + dot(left, right, 0, 0)
        pre = both[0:64, 0:SPAN] + both[64:SPAN, SPAN:] + bias1[pl.ds(g, 1), :]
        hidden = jnp.maximum(pre, 0.0).astype(bf16)
        top_mean = (dot(picked, hidden) / top_div).astype(bf16)
        span = pl.ds(pl.multiple_of(g * SPAN, SPAN), SPAN)
        w2s_g = w2s[:, span]
        w2n_g = w2n[:, span]
        part = dot(hidden, w2s_g, 1, 1) + dot(top_mean, w2n_g, 1, 1)
        lp[:, :, 0:CLASSES] = part.reshape(NG, 8, CLASSES)
        launch("lr", NG, to_g, lambda p: lp.at[(g + p) % NG], lr.at[g], lambda p: lr.at[g_of(p)])
        lr[g] = lp[g]
    with jax.named_scope("logits_wait"):
        depart()
        arrive("lr")

    with jax.named_scope("softmax"):
        logits = jnp.sum(lr[...], axis=0)[:, 0:CLASSES] + bias2[...]
        exps = jnp.exp(logits)
        total = jnp.sum(exps, axis=1, keepdims=True)
        onehot = jnp.where(iota((8, CLASSES), 1).astype(f32) == label_col, 1.0, 0.0)
        row_loss = jnp.log(total) - jnp.sum(onehot * logits, axis=1, keepdims=True)
        grad = ((exps / total - onehot) * (loss_scale / TARGETS)).astype(bf16)
        gl_src[...] = jnp.where(iota((8, 2 * SPAN), 1) == LOSS_LANE, row_loss, 0.0)
        gl_src[:, 0:CLASSES] = grad.astype(f32)
        launch("gl", NG, to_g, lambda p: gl_src, gl_all.at[g], lambda p: gl_all.at[g_of(p)])
        gl_all[g] = gl_src[...]
        g2[...] = jnp.zeros_like(g2)
    with jax.named_scope("grad_logits_wait"):
        arrive("gl")

    with jax.named_scope("classifier_grads"):
        gl_rows = gl_all[...].reshape(64, 2 * SPAN)
        gl = gl_rows[:, 0:CLASSES].astype(bf16)
        g2[0:CLASSES, :] = dot(gl, hidden, 0, 0)
        g2[NBR_AT:NBR_AT + CLASSES, :] = dot(gl, top_mean, 0, 0)
        col_sums = jnp.sum(gl_rows, axis=0, keepdims=True)
        g2[TAIL_AT:TAIL_AT + 1, :] = col_sums[:, 0:SPAN]
        g2[TAIL_AT + 1:TAIL_AT + 2, :] = col_sums[:, SPAN:]

        def block(r, d):
            return g2.at[pl.ds(pl.multiple_of((d * 4 + r) * BLOCK, 8), BLOCK)]

        def scatter(act, wait=False):
            for i, p in enumerate(NEAR):
                def run(q, i=i, p=p):
                    device = {"cols": ((z + p) % NZ) * NG + g, "rep": (y + q) % NY}
                    got = ra.at[i, y_of(q)] if wait else ra.at[i, y]
                    act(copy("scatter", i * 4 + q, block((z + p) % 4, (y + q) % NY), got, device))

                each(NY, run, 0 if i else 1)

        scatter(lambda send: send.start())
        departures.append(lambda: scatter(lambda send: send.wait_send()))
        ra[0, y] = g2[pl.ds(pl.multiple_of((y * 4 + row) * BLOCK, 8), BLOCK), :]

    with jax.named_scope("back"):
        back_top = dot(gl, w2n_g) / top_div
        top_1 = back_top.astype(bf16)
        rest = back_top - top_1.astype(f32)
        top_2 = rest.astype(bf16)
        top_3 = (rest - top_2.astype(f32)).astype(bf16)
        back = dot(gl, w2s_g) + (dot(picked, top_1, 0, 0) + (dot(picked, top_2, 0, 0) + dot(picked, top_3, 0, 0)))
        grad_pre = jnp.where(pre > 0.0, back, 0.0).astype(bf16)
        gp_all[row, col] = grad_pre
        mine_gp = gp_all.at[row, col]
        launch("gp_far", 4, to_far, lambda p: mine_gp, mine_gp, lambda p: gp_all.at[row, far_of(p)])
        launch("xg", NG, to_g, lambda p: xp, xg.at[g], lambda p: xg.at[g_of(p)])

    with jax.named_scope("scatter"):
        scatter(lambda send: send.wait_recv(), wait=True)
        rb[col] = jnp.sum(ra[...].reshape(4 * NY, BLOCK, SPAN), axis=0)
        mine_rb = rb.at[col]
        launch("far", 4, to_far, lambda p: mine_rb, mine_rb, lambda p: rb.at[far_of(p)])

    with jax.named_scope("grad_pre_far"):
        arrive("gp_far")
        launch_near("gp_near", gp_all.at[row], gp_all.at[row], lambda r: gp_all.at[r])

    with jax.named_scope("far"):
        arrive("far")
        rc[row] = jnp.sum(rb[...], axis=0)
        launch_near("near", rc.at[row], rc.at[row], lambda r: rc.at[r])

    with jax.named_scope("gather_over_z"):
        arrive("near")
        earlier = departures[:]
        departures.clear()
        fin = rc[...].reshape(PART, SPAN)
        low_part = fin - fin.astype(bf16).astype(f32)
        low_part = jnp.concatenate([low_part[0:2], low_part[0:PART - 2]], axis=0)
        at = iota((PART, SPAN), 0) - (TAIL_AT - (NY - 1) * PART)
        is_low = (y == NY - 1) & (at >= 2) & (at < 4)
        spread[x, y] = jnp.where(is_low, low_part, fin).astype(bf16)
        out_block = spread.at[x, y]
        each(NP, lambda p: copy("plane", p, out_block, out_block, to_plane(p)).start())

        def keep(q):
            return pltpu.make_async_copy(spread.at[q // NY, q % NY], full.at[c, q // NY, q % NY], keep_sem.at[q])

        def to_other_core(q):
            return copy("core", q, spread.at[q // NY, q % NY], full.at[c, q // NY, q % NY], to_core)

        keep(here).start()
        to_other_core(here).start()

    with jax.named_scope("grad_pre_near"):
        arrive("xg")
        arrive("gp_near")
    with jax.named_scope("layer_grads"):
        dw = jnp.zeros((SPAN, SPAN), f32)
        for t in range(8):
            pair = [gp_all[(2 * t + i) % 4, (2 * t + i) // 4] for i in range(2)]
            dw = dw + dot(xg[:, t].reshape(SPAN, SPAN), jnp.concatenate(pair, axis=0))
        dw_src[...] = dw.reshape(NG, 16, SPAN)
        launch("dw", NG, to_g, lambda p: dw_src.at[(g + p) % NG], dw_in.at[g], lambda p: dw_in.at[g_of(p)])
        dw_in[g] = dw_src[g]

    with jax.named_scope("layer_grads_wait"):
        arrive("dw")
        y2[y] = dw_in[...].astype(bf16)
        launch("y2", NY, to_y, lambda p: y2.at[y], y2.at[y], lambda p: y2.at[y_of(p)])

    with jax.named_scope("gather_over_plane"):
        for wait in earlier:
            wait()

        def forward(p):
            q = (here + NP - p) % NP
            copy("plane", p, out_block, spread.at[q // NY, q % NY], to_plane(p)).wait_recv()
            to_other_core(q).start()
            keep(q).start()

        each(NP, forward)
        departures.append(lambda: each(NP, lambda p: copy("plane", p, out_block, out_block, to_plane(p)).wait_send()))
        departures.append(lambda: each(NP, lambda q: to_other_core(q).wait_send(), 0))
        departures.append(lambda: each(NP, lambda q: keep(q).wait(), 0))

    with jax.named_scope("layer_grads_over_rep"):
        arrive("y2")
        g1_out[...] = jnp.sum(y2[...].astype(f32), axis=0)

    with jax.named_scope("gather_over_core"):
        def from_core(q):
            copy("core", q, spread.at[q // NY, q % NY], full.at[1 - c, q // NY, q % NY], to_core).wait_recv()

        each(NP, from_core, 0)

    with jax.named_scope("sends"):
        depart()


def finish_kernel(full_hbm, g1_hbm, *refs):
    outs, bufs, full, g1, load_sem, sem = refs[0:7], refs[7:14], refs[14], refs[15], refs[16], refs[17]
    loss, g1s, g1n, gb1, g2s, g2n, gb2 = bufs
    blocks = [
        pltpu.make_async_copy(full_hbm.at[d % 2, d // 2], full.at[d % 2, d // 2], load_sem.at[d]) for d in range(NG)
    ]
    small = pltpu.make_async_copy(g1_hbm, g1, load_sem.at[NG])
    small.start()
    for block in blocks:
        block.start()
    small.wait()
    for d in range(NG):
        cut = slice(d * SPAN, (d + 1) * SPAN)
        g1s[:, cut] = g1[d, 0:COLS]
        g1n[:, cut] = g1[d, COLS:2 * COLS]
        gb1[d:d + 1, :] = g1[d, 2 * COLS:2 * COLS + 1]
    blocks[0].wait()
    rows = full[0, 0, NY - 1].astype(f32)
    at = TAIL_AT - (NY - 1) * PART
    tail = rows[at:at + 2] + rows[at + 2:at + 4]
    gb2[:, 0:SPAN] = tail[0:1]
    gb2[:, SPAN:CLASSES] = tail[1:2, 0:CLASSES - SPAN]
    loss[...] = tail[1:2, LOSS_LANE - SPAN:LOSS_LANE - SPAN + 1] / TARGETS
    stores = []

    def store(src, dst):
        stores.append(pltpu.make_async_copy(src, dst, sem.at[len(stores)]))
        stores[-1].start()

    for i in (0, 1, 2, 3, 6):
        store(bufs[i], outs[i])
    for d in range(NG):
        cut = slice(d * SPAN, (d + 1) * SPAN)
        if d:
            blocks[d].wait()
        flat = full[d % 2, d // 2].astype(f32).reshape(GRAD_ROWS, SPAN)
        g2s[:, cut] = flat[0:CLASSES]
        g2n[:, cut] = flat[NBR_AT:NBR_AT + CLASSES]
        store(g2s.at[:, cut], outs[4].at[:, cut])
        store(g2n.at[:, cut], outs[5].at[:, cut])
    for copied in stores:
        copied.wait()


def per_device(
    features, self_ids, nbr_ids, nbr_counts, w1_self, w1_nbr, bias1, w2_self, w2_nbr, bias2, labels, top_ids, top_counts
):
    hidden = bias1.shape[0]
    operands = (
        features.T, self_ids.T, jnp.transpose(nbr_ids, (2, 1, 0)), nbr_counts.T, w1_self, w1_nbr,
        bias1.reshape(NG, SPAN), w2_self.T, w2_nbr.T, bias2.reshape(1, CLASSES), labels.reshape(1, 8),
        top_ids, top_counts.reshape(1, 8),
    )
    scratch = [VMEM(a.shape, a.dtype) for a in operands] + [
        VMEM((LOW // SPAN, HIGH * 8, SPAN), f32),
        VMEM((HIGH * COLS, LOW), bf16),
        VMEM((16, hidden), f32),
        VMEM((NG, 16, SPAN), bf16),
        VMEM((NG, 16, SPAN), bf16),
        VMEM((4, 4, SPAN, SPAN), bf16),
        VMEM((NG, 8, SPAN), f32),
        VMEM((8, SPAN, SPAN), f32),
        VMEM((8 * SPAN, SPAN), f32),
        VMEM((8, 16, SPAN), bf16),
        VMEM((NZ, 16, SPAN), bf16),
        VMEM((NZ, 16, SPAN), bf16),
        VMEM((2, 4, 16, SPAN), bf16),
        VMEM((NG, 2, 4, 16, SPAN), bf16),
        VMEM((NG, 8, 16, SPAN), bf16),
        VMEM((NG, 8, 2 * SPAN), f32),
        VMEM((NG, 8, 2 * SPAN), f32),
        VMEM((8, 2 * SPAN), f32),
        VMEM((NG, 8, 2 * SPAN), f32),
        VMEM((4, 4, 64, SPAN), bf16),
        VMEM((GRAD_ROWS, SPAN), f32),
        VMEM((4, NY, BLOCK, SPAN), f32),
        VMEM((4, BLOCK, SPAN), f32),
        VMEM((4, BLOCK, SPAN), f32),
        VMEM((NX, NY, PART, SPAN), bf16),
        VMEM((NG, 16, SPAN), f32),
        VMEM((NG, 16, SPAN), f32),
        VMEM((NY, NG, 16, SPAN), bf16),
        pltpu.SemaphoreType.DMA((total_sems,)),
        pltpu.SemaphoreType.DMA((total_sems,)),
        pltpu.SemaphoreType.DMA((len(operands),)),
        pltpu.SemaphoreType.DMA((NP,)),
    ]
    full, g1 = pl.pallas_call(
        step_kernel,
        out_shape=[
            jax.ShapeDtypeStruct((2, NX, NY, PART, SPAN), bf16), jax.ShapeDtypeStruct((NG, 16, SPAN), f32),
        ],
        in_specs=[pl.BlockSpec(memory_space=pltpu.HBM)] * len(operands),
        out_specs=[pl.BlockSpec(memory_space=pltpu.HBM), pl.BlockSpec(memory_space=VMEM)],
        scratch_shapes=scratch,
        compiler_params=pltpu.CompilerParams(
            collective_id=0, has_side_effects=True, vmem_limit_bytes=60 * 2**20
        ),
        name="step",
    )(*operands)
    shapes = (
        (1, 1), (COLS, hidden), (COLS, hidden), (NG, SPAN), (CLASSES, hidden), (CLASSES, hidden), (1, CLASSES),
    )
    loss, g1s, g1n, gb1, g2s, g2n, gb2 = pl.pallas_call(
        finish_kernel,
        out_shape=[jax.ShapeDtypeStruct(s, f32) for s in shapes],
        in_specs=[pl.BlockSpec(memory_space=pltpu.HBM)] * 2,
        out_specs=[pl.BlockSpec(memory_space=pltpu.HBM)] * len(shapes),
        scratch_shapes=[VMEM(s, f32) for s in shapes] + [
            VMEM(full.shape, bf16), VMEM(g1.shape, f32),
            pltpu.SemaphoreType.DMA((NG + 1,)), pltpu.SemaphoreType.DMA((5 + 2 * NG,)),
        ],
        compiler_params=pltpu.CompilerParams(vmem_limit_bytes=60 * 2**20),
        name="finish",
    )(full, g1)
    return loss.reshape(()), g1s, g1n, gb1.reshape(hidden), g2s.T, g2n.T, gb2.reshape(CLASSES)


def solution(mesh):
    in_specs = (
        P(None, "cols"), P(None, "rep"), P(None, "rep", None), P(None, "rep"), P("cols", None), P("cols", None),
        P(), P(), P(), P(), P(("cols", "rep")), P(("cols", "rep"), None), P(("cols", "rep")),
    )
    out_specs = (P(), P("cols", None), P("cols", None), P(), P(), P(), P())
    return jax.shard_map(per_device, mesh=mesh, in_specs=in_specs, out_specs=out_specs, check_vma=False)
```

```python
import jax
import jax.numpy as jnp
from jax import lax
from jax.experimental import pallas as pl
from jax.experimental.pallas import tpu as pltpu
from jax.sharding import PartitionSpec as P

f32, bf16 = jnp.float32, jnp.bfloat16
loss_scale = 64.0

NZ, NG, NY, NX = 16, 8, 4, 4
TARGETS = 8 * NZ * NG * NY
LOW = 512
HIGH = 65536 // LOW
COLS = 6
FAN = 25
CLASSES = 153
LOSS_LANE = 200
SPAN = 128
NP = NX * NY
NBR_AT = 159
TAIL_AT = 312
GRAD_ROWS = 384
PART = GRAD_ROWS // NY
BLOCK = PART // 4
NEAR = (0, 1, NZ - 1, 2)
VMEM = pltpu.VMEM

SEMS = {}
total_sems = 0
for stage, slots in (
    ("w_g", NG), ("aux", NG), ("w_far", 4), ("w_near", 4), ("x_z", NZ), ("x_g0", NG), ("x_g1", NG), ("xg", NG), ("lr", NG), ("gl", NG),
    ("gp_far", 4), ("gp_near", 4), ("scatter", 16), ("far", 4), ("near", 4), ("plane", NP), ("core", NP),
    ("dw", NG), ("y2", NY),
):
    SEMS[stage] = total_sems
    total_sems += slots


def dot(a, b, ca=1, cb=0):
    return lax.dot_general(a, b, (((ca,), (cb,)), ((), ())), preferred_element_type=f32)


def iota(shape, dim):
    return lax.broadcasted_iota(jnp.int32, shape, dim)


def step_kernel(
    feat_hbm, self_hbm, nbr_hbm, counts_hbm, w1s_hbm, w1n_hbm, bias1_hbm, w2s_hbm, w2n_hbm, bias2_hbm, labels_hbm,
    top_hbm, top_counts_hbm, full, g1_out,
    feat, self_ids, nbr_ids, nbr_counts, w1s, w1n, bias1, w2s, w2n, bias2, labels, top_ids, top_counts,
    split, table, wt, w_src, w_mid, w_all, aux, rows_t, rows_m, xp, x_src, x_in, x_mid, x_all, xg,
    lp, lr, gl_src, gl_all, gp_all, g2, ra, rb, rc, spread, dw_src, dw_in, y2, send_sem, recv_sem, load_sem, keep_sem,
):
    o = lax.axis_index("cols")
    y = lax.axis_index("rep")
    z = o // NG
    g = o % NG
    x = g // 2
    c = g % 2
    here = x * NY + y

    def to_z(p):
        return {"cols": ((z + p) % NZ) * NG + g, "rep": y}

    def to_g(p):
        return {"cols": z * NG + (g + p) % NG, "rep": y}

    def to_y(p):
        return {"cols": o, "rep": (y + p) % NY}

    def to_plane(p):
        return {"cols": z * NG + ((x + p // NY) % NX) * 2 + c, "rep": (y + p % NY) % NY}

    def plane_of(p):
        return (x + NX - p // NY) % NX, (y + NY - p % NY) % NY

    def ring(step, n):
        return min(step % n, -step % n)

    plane_steps = sorted(range(1, NP), key=lambda p: -(ring(p // NY, NX) + ring(p % NY, NY)))

    to_core = {"cols": z * NG + x * 2 + (1 - c), "rep": y}

    def copy(stage, p, src, dst, device):
        at = SEMS[stage] + p
        return pltpu.make_async_remote_copy(
            src_ref=src, dst_ref=dst, send_sem=send_sem.at[at], recv_sem=recv_sem.at[at], device_id=device
        )

    def each(n, body, first=1):
        def run(p, carry):
            body(p)
            return carry
        lax.fori_loop(first, n, run, 0)

    arrivals, departures = {}, []

    def launch(stage, n, device, src, dst, got):
        for p in sorted(range(1, n), key=lambda p: abs(p - n // 2)):
            copy(stage, p, src(p), dst, device(p)).start()

        def wait_all():
            for p in range(1, n):
                copy(stage, p, src(p), got(p), device(p)).wait_recv()

        arrivals[stage] = wait_all
        departures.append(lambda: each(n, lambda p: copy(stage, p, src(p), dst, device(p)).wait_send()))

    def launch_near(stage, src, dst, got):
        steps = list(enumerate(NEAR))[1:]
        for i, p in steps:
            copy(stage, i, src, dst, to_z(p)).start()

        def wait_near():
            for i, p in steps:
                copy(stage, i, src, got((z + NZ - p) % 4), to_z(p)).wait_recv()

        def sent_near():
            for i, p in steps:
                copy(stage, i, src, dst, to_z(p)).wait_send()

        arrivals[stage] = wait_near
        departures.append(sent_near)

    def arrive(stage):
        arrivals.pop(stage)()

    def depart():
        while departures:
            departures.pop(0)()

    def to_far(p):
        return to_z(4 * p)

    row, col = z % 4, z // 4

    def far_of(p):
        return (col + 4 - p) % 4

    def z_of(p):
        return (z + NZ - p) % NZ

    def g_of(p):
        return (g + NG - p) % NG

    def y_of(p):
        return (y + NY - p) % NY

    loads = [
        pltpu.make_async_copy(src, dst, load_sem.at[i])
        for i, (src, dst) in enumerate((
            (feat_hbm, feat), (w1s_hbm, w1s), (w1n_hbm, w1n), (top_counts_hbm, top_counts), (labels_hbm, labels),
            (top_hbm, top_ids), (self_hbm, self_ids), (counts_hbm, nbr_counts), (nbr_hbm, nbr_ids),
            (bias1_hbm, bias1), (bias2_hbm, bias2), (w2s_hbm, w2s), (w2n_hbm, w2n),
        ))
    ]
    for load in loads:
        load.start()
    waiting = list(range(13))

    def ready(first, last):
        for i in range(first, last):
            waiting.remove(i)
            loads[i].wait()

    barrier = pltpu.get_barrier_semaphore()
    others = [to_z(p) for p in sorted(range(1, NZ), key=lambda p: abs(p - NZ // 2))]
    others += [
        {"cols": ((z + step) % NZ) * NG + g, "rep": (y + p) % NY} for step in NEAR[1:] + (NZ - 2,) for p in range(1, NY)
    ]
    others += [{"cols": z * NG + i * 2 + c, "rep": (y + p) % NY} for i in range(NX) for p in range(1, NY)]
    others += [to_g(p) for p in range(1, NG)]
    n_others = len(others)

    def greet(n):
        for device in others[:n]:
            pl.semaphore_signal(barrier, inc=1, device_id=device)
        del others[:n]

    greet(NZ - 1)

    with jax.named_scope("prepare"):
        wt[...] = jnp.zeros_like(wt)
        ready(1, 6)
        wt[0:COLS, :] = w1s[...].astype(f32)
        wt[COLS:2 * COLS, :] = w1n[...].astype(f32)
        for d in range(NG):
            w_src[d] = wt[:, d * SPAN:(d + 1) * SPAN].astype(bf16)
        w_mid[g] = w_src[g]

        eye = iota((8, 8), 0) == iota((8, 8), 1)

        def column(ref):
            return jnp.sum(jnp.where(eye, jnp.broadcast_to(ref[...].astype(f32), (8, 8)), 0.0), axis=1, keepdims=True)

        count_col = column(top_counts)
        label_col = column(labels)
        picks = top_ids[...]
        live_top = iota(picks.shape, 1).astype(f32) < count_col
        lane = iota((8, SPAN), 1)
        mine = jnp.where(lane == 8, count_col, jnp.where(lane == 9, label_col, 0.0))
        for s in range(8):
            n_s = jnp.sum(jnp.where(live_top & (picks == s), 1.0, 0.0), axis=1, keepdims=True)
            mine = jnp.where(lane == s, n_s, mine)
        aux[g] = mine

    with jax.named_scope("table"):
        ready(0, 1)

        for h in range(HIGH):
            piece = feat[:, h * LOW:(h + 1) * LOW].astype(f32)
            for q in range(LOW // SPAN):
                split[q, h * 8:h * 8 + COLS, :] = piece[:, q * SPAN:(q + 1) * SPAN]
            if h % 3 == 2:
                greet(1)
        greet(len(others))
        for k in range(COLS):
            for q in range(LOW // SPAN):
                table[k * HIGH:(k + 1) * HIGH, q * SPAN:(q + 1) * SPAN] = (
                    split[q, pl.ds(k, HIGH, stride=8), :].astype(bf16)
                )

    with jax.named_scope("lookup"):
        ready(6, 9)
        io_low = iota((256, SPAN), 0).astype(f32).astype(bf16)
        io_high = iota((HIGH, SPAN), 0)
        counts = nbr_counts[...]

        def look(ids, alive):
            low = jnp.bitwise_and(ids, LOW - 1).astype(f32)
            high = jnp.where(alive, jnp.right_shift(ids, LOW.bit_length() - 1), -1)

            def hot_rows(first, j):
                at = jnp.broadcast_to((low[j:j + 1, :] - first).astype(bf16), (256, SPAN))
                return jnp.where(io_low == at, jnp.bfloat16(1), jnp.bfloat16(0))

            hot = jnp.concatenate([
                jnp.concatenate([hot_rows(float(first), j) for j in range(8)], axis=1) for first in range(0, LOW, 256)
            ], axis=0)
            mask = jnp.concatenate([io_high == high[j:j + 1, :] for j in range(8)], axis=1)
            got = dot(table[...], hot)
            found = []
            for k in range(COLS):
                one = jnp.zeros((8, 8 * SPAN), f32)
                for b in range(0, HIGH, 8):
                    one = jnp.where(mask[b:b + 8], got[k * HIGH + b:k * HIGH + b + 8], one)
                found.append(one)
            return tuple(found)

        def add_nbr(k, sums):
            return tuple(a + b for a, b in zip(sums, look(nbr_ids[k], counts > k)))

        own = look(self_ids[...], counts > 0)
        pl.semaphore_wait(barrier, n_others)
        launch("w_g", NG, to_g, lambda p: w_src.at[(g + p) % NG], w_mid.at[g], lambda p: w_mid.at[g_of(p)])
        launch("aux", NG, to_g, lambda p: aux.at[g], aux.at[g], lambda p: aux.at[g_of(p)])
        sums = tuple(jnp.zeros((8, 8 * SPAN), f32) for _ in range(COLS))
        sums = lax.fori_loop(0, 5, add_nbr, sums, unroll=5)
        arrive("w_g")
        w_all[row, col] = w_mid[...].reshape(SPAN, SPAN)
        w_mine = w_all.at[row, col]
        launch("w_far", 4, to_far, lambda p: w_mine, w_mine, lambda p: w_all.at[row, far_of(p)])
        sums = lax.fori_loop(5, 15, add_nbr, sums, unroll=5)
        arrive("w_far")
        launch_near("w_near", w_all.at[row], w_all.at[row], lambda r: w_all.at[r])
        sums = lax.fori_loop(15, FAN, add_nbr, sums, unroll=5)

    with jax.named_scope("rows"):
        rows_t[...] = jnp.zeros_like(rows_t)
        for j in range(8):
            cut = slice(j * SPAN, (j + 1) * SPAN)
            count = counts[j:j + 1, :].astype(f32)
            for k in range(COLS):
                rows_t[j, k:k + 1, :] = jnp.sum(own[k][:, cut], axis=0, keepdims=True)
                rows_t[j, COLS + k:COLS + k + 1, :] = jnp.sum(sums[k][:, cut], axis=0, keepdims=True) / count
            rows_t[j, 2 * COLS:2 * COLS + 1, :] = jnp.ones((1, SPAN), f32)
        for j in range(8):
            rows_m[pl.ds(j, SPAN, stride=8), :] = rows_t[j].T
        for t in range(8):
            xp[t] = rows_m[t * SPAN:(t + 1) * SPAN, :].T[0:16, :].astype(bf16)

        odd = z % 2
        half = iota((16, SPAN), 1) // 64
        for t in range(8):
            straight = xp[t].astype(f32)
            turned = pltpu.roll(straight, 64, 1)
            x_src[2 * t] = jnp.where(half == odd, jnp.where(odd == 0, straight, turned), 0.0).astype(bf16)
            x_src[2 * t + 1] = jnp.where(half == odd, jnp.where(odd == 1, straight, turned), 0.0).astype(bf16)
        launch("x_z", NZ, to_z, lambda p: x_src.at[(z + p) % NZ], x_in.at[z], lambda p: x_in.at[z_of(p)])
        x_in[z] = x_src[z]
        xg[g] = xp[...]

    with jax.named_scope("lists"):
        arrive("aux")
        lists = aux[...].reshape(64, SPAN)
        top_div = lists[:, 8:9]
        repeat = (iota((SPAN, 64), 0) == iota((SPAN, 64), 1) % 8).astype(f32).astype(bf16)
        same = iota((64, 64), 0) // 8 == iota((64, 64), 1) // 8
        picked = jnp.where(same, dot(lists.astype(bf16), repeat), 0.0).astype(bf16)
        ready(9, 13)
        lp[...] = jnp.zeros_like(lp)

    with jax.named_scope("rows_to_z"):
        arrive("w_near")
        arrivals.pop("x_z")
        pairs = [(z // 2 + p) % 8 for p in (0, 1, 7, 2, 6, 3, 5, 4)]

        def z_pair(i):
            for odd_z in range(2):
                if i == 0 and odd_z:
                    continue
                source = 2 * pairs[i] + odd_z if i else 2 * pairs[0] + 1 - odd
                copy("x_z", (z + NZ - source) % NZ, x_src.at[0], x_in.at[source], to_z(1)).wait_recv()
            x_mid[i // 4, i % 4] = x_in[2 * pairs[i]] + x_in[2 * pairs[i] + 1]

        for half_z in range(2):
            for i in range(4):
                z_pair(4 * half_z + i)
            launch(
                f"x_g{half_z}", NG, to_g, lambda p, h=half_z: x_mid.at[h], x_all.at[g, half_z],
                lambda p, h=half_z: x_all.at[g_of(p), h],
            )
        x_all[g] = x_mid[...]

    with jax.named_scope("rows_over_g"):
        depart()
        arrive("x_g0")
        arrive("x_g1")
    with jax.named_scope("layers"):
        both = jnp.zeros((SPAN, 2 * SPAN), f32)
        for t in range(8):
            left = x_all[:, t // 4, t % 4].reshape(SPAN, SPAN)
            sources = [2 * pairs[t] + i for i in range(2)]
            right = jnp.concatenate([w_all[source % 4, source // 4] for source in sources], axis=1)
            both = both + dot(left, right, 0, 0)
        pre = both[0:64, 0:SPAN] + both[64:SPAN, SPAN:] + bias1[pl.ds(g, 1), :]
        hidden = jnp.maximum(pre, 0.0).astype(bf16)
        top_mean = (dot(picked, hidden) / top_div).astype(bf16)
        span = pl.ds(pl.multiple_of(g * SPAN, SPAN), SPAN)
        w2s_g = w2s[:, span]
        w2n_g = w2n[:, span]
        part = dot(hidden, w2s_g, 1, 1) + dot(top_mean, w2n_g, 1, 1)
        lp[:, :, 0:CLASSES] = part.reshape(NG, 8, CLASSES)
        launch("lr", NG, to_g, lambda p: lp.at[(g + p) % NG], lr.at[g], lambda p: lr.at[g_of(p)])
        lr[g] = lp[g]
    with jax.named_scope("logits_wait"):
        depart()
        arrive("lr")

    with jax.named_scope("softmax"):
        logits = jnp.sum(lr[...], axis=0)[:, 0:CLASSES] + bias2[...]
        exps = jnp.exp(logits)
        total = jnp.sum(exps, axis=1, keepdims=True)
        onehot = jnp.where(iota((8, CLASSES), 1).astype(f32) == label_col, 1.0, 0.0)
        row_loss = jnp.log(total) - jnp.sum(onehot * logits, axis=1, keepdims=True)
        grad = ((exps / total - onehot) * (loss_scale / TARGETS)).astype(bf16)
        gl_src[...] = jnp.where(iota((8, 2 * SPAN), 1) == LOSS_LANE, row_loss, 0.0)
        gl_src[:, 0:CLASSES] = grad.astype(f32)
        launch("gl", NG, to_g, lambda p: gl_src, gl_all.at[g], lambda p: gl_all.at[g_of(p)])
        gl_all[g] = gl_src[...]
        g2[...] = jnp.zeros_like(g2)
    with jax.named_scope("grad_logits_wait"):
        arrive("gl")

    with jax.named_scope("classifier_grads"):
        gl_rows = gl_all[...].reshape(64, 2 * SPAN)
        gl = gl_rows[:, 0:CLASSES].astype(bf16)
        g2[0:CLASSES, :] = dot(gl, hidden, 0, 0)
        g2[NBR_AT:NBR_AT + CLASSES, :] = dot(gl, top_mean, 0, 0)
        col_sums = jnp.sum(gl_rows, axis=0, keepdims=True)
        g2[TAIL_AT:TAIL_AT + 1, :] = col_sums[:, 0:SPAN]
        g2[TAIL_AT + 1:TAIL_AT + 2, :] = col_sums[:, SPAN:]

        def block(r, d):
            return g2.at[pl.ds(pl.multiple_of((d * 4 + r) * BLOCK, 8), BLOCK)]

        def scatter(act, wait=False):
            steps = [(i, q) for i in range(4) for q in range(NY) if i or q]
            for i, q in sorted(steps, key=lambda iq: -(ring(NEAR[iq[0]], NZ) + ring(iq[1], NY))):
                device = {"cols": ((z + NEAR[i]) % NZ) * NG + g, "rep": (y + q) % NY}
                got = ra.at[i, y_of(q)] if wait else ra.at[i, y]
                act(copy("scatter", i * 4 + q, block((z + NEAR[i]) % 4, (y + q) % NY), got, device))

        scatter(lambda send: send.start())
        departures.append(lambda: scatter(lambda send: send.wait_send()))
        ra[0, y] = g2[pl.ds(pl.multiple_of((y * 4 + row) * BLOCK, 8), BLOCK), :]

    with jax.named_scope("back"):
        back_top = dot(gl, w2n_g) / top_div
        top_1 = back_top.astype(bf16)
        rest = back_top - top_1.astype(f32)
        top_2 = rest.astype(bf16)
        top_3 = (rest - top_2.astype(f32)).astype(bf16)
        back = dot(gl, w2s_g) + (dot(picked, top_1, 0, 0) + (dot(picked, top_2, 0, 0) + dot(picked, top_3, 0, 0)))
        grad_pre = jnp.where(pre > 0.0, back, 0.0).astype(bf16)
        gp_all[row, col] = grad_pre
        mine_gp = gp_all.at[row, col]
        launch("gp_far", 4, to_far, lambda p: mine_gp, mine_gp, lambda p: gp_all.at[row, far_of(p)])
        launch("xg", NG, to_g, lambda p: xp, xg.at[g], lambda p: xg.at[g_of(p)])

    with jax.named_scope("scatter"):
        scatter(lambda send: send.wait_recv(), wait=True)
        rb[col] = jnp.sum(ra[...].reshape(4 * NY, BLOCK, SPAN), axis=0)
        mine_rb = rb.at[col]
        launch("far", 4, to_far, lambda p: mine_rb, mine_rb, lambda p: rb.at[far_of(p)])

    with jax.named_scope("grad_pre_far"):
        arrive("gp_far")
        launch_near("gp_near", gp_all.at[row], gp_all.at[row], lambda r: gp_all.at[r])

    with jax.named_scope("far"):
        arrive("far")
        rc[row] = jnp.sum(rb[...], axis=0)
        launch_near("near", rc.at[row], rc.at[row], lambda r: rc.at[r])

    with jax.named_scope("gather_over_z"):
        arrive("near")
        earlier = departures[:]
        departures.clear()
        fin = rc[...].reshape(PART, SPAN)
        low_part = fin - fin.astype(bf16).astype(f32)
        low_part = jnp.concatenate([low_part[0:2], low_part[0:PART - 2]], axis=0)
        at = iota((PART, SPAN), 0) - (TAIL_AT - (NY - 1) * PART)
        is_low = (y == NY - 1) & (at >= 2) & (at < 4)
        spread[x, y] = jnp.where(is_low, low_part, fin).astype(bf16)
        out_block = spread.at[x, y]
        for p in plane_steps:
            copy("plane", p, out_block, out_block, to_plane(p)).start()

        def keep(q):
            return pltpu.make_async_copy(spread.at[q // NY, q % NY], full.at[c, q // NY, q % NY], keep_sem.at[q])

        def to_other_core(q):
            return copy("core", q, spread.at[q // NY, q % NY], full.at[c, q // NY, q % NY], to_core)

        keep(here).start()
        to_other_core(here).start()

    with jax.named_scope("grad_pre_near"):
        arrive("xg")
        arrive("gp_near")
    with jax.named_scope("layer_grads"):
        dw = jnp.zeros((SPAN, SPAN), f32)
        for t in range(8):
            pair = [gp_all[(2 * t + i) % 4, (2 * t + i) // 4] for i in range(2)]
            dw = dw + dot(xg[:, t].reshape(SPAN, SPAN), jnp.concatenate(pair, axis=0))
        dw_src[...] = dw.reshape(NG, 16, SPAN)
        launch("dw", NG, to_g, lambda p: dw_src.at[(g + p) % NG], dw_in.at[g], lambda p: dw_in.at[g_of(p)])
        dw_in[g] = dw_src[g]

    with jax.named_scope("layer_grads_wait"):
        arrive("dw")
        y2[y] = dw_in[...].astype(bf16)
        launch("y2", NY, to_y, lambda p: y2.at[y], y2.at[y], lambda p: y2.at[y_of(p)])

    with jax.named_scope("gather_over_plane"):
        for wait in earlier:
            wait()

        for p in plane_steps:
            x_from, y_from = plane_of(p)
            copy("plane", p, out_block, spread.at[x_from, y_from], to_plane(p)).wait_recv()
            to_other_core(x_from * NY + y_from).start()
            keep(x_from * NY + y_from).start()

        departures.append(lambda: each(NP, lambda p: copy("plane", p, out_block, out_block, to_plane(p)).wait_send()))
        departures.append(lambda: each(NP, lambda q: to_other_core(q).wait_send(), 0))
        departures.append(lambda: each(NP, lambda q: keep(q).wait(), 0))

    with jax.named_scope("layer_grads_over_rep"):
        depart()
        arrive("y2")
        g1_out[...] = jnp.sum(y2[...].astype(f32), axis=0)

    with jax.named_scope("gather_over_core"):
        def from_core(q):
            copy("core", q, spread.at[q // NY, q % NY], full.at[1 - c, q // NY, q % NY], to_core).wait_recv()

        each(NP, from_core, 0)


def finish_kernel(full_hbm, g1_hbm, *refs):
    outs, bufs, full, g1, load_sem, sem = refs[0:7], refs[7:14], refs[14], refs[15], refs[16], refs[17]
    loss, g1s, g1n, gb1, g2s, g2n, gb2 = bufs
    blocks = [
        pltpu.make_async_copy(full_hbm.at[d % 2, d // 2], full.at[d % 2, d // 2], load_sem.at[d]) for d in range(NG)
    ]
    small = pltpu.make_async_copy(g1_hbm, g1, load_sem.at[NG])
    small.start()
    for block in blocks:
        block.start()
    small.wait()
    for d in range(NG):
        cut = slice(d * SPAN, (d + 1) * SPAN)
        g1s[:, cut] = g1[d, 0:COLS]
        g1n[:, cut] = g1[d, COLS:2 * COLS]
        gb1[d:d + 1, :] = g1[d, 2 * COLS:2 * COLS + 1]
    blocks[0].wait()
    rows = full[0, 0, NY - 1].astype(f32)
    at = TAIL_AT - (NY - 1) * PART
    tail = rows[at:at + 2] + rows[at + 2:at + 4]
    gb2[:, 0:SPAN] = tail[0:1]
    gb2[:, SPAN:CLASSES] = tail[1:2, 0:CLASSES - SPAN]
    loss[...] = tail[1:2, LOSS_LANE - SPAN:LOSS_LANE - SPAN + 1] / TARGETS
    stores = []

    def store(src, dst):
        stores.append(pltpu.make_async_copy(src, dst, sem.at[len(stores)]))
        stores[-1].start()

    for i in (0, 1, 2, 3, 6):
        store(bufs[i], outs[i])
    for d in range(NG):
        cut = slice(d * SPAN, (d + 1) * SPAN)
        if d:
            blocks[d].wait()
        flat = full[d % 2, d // 2].astype(f32).reshape(GRAD_ROWS, SPAN)
        g2s[:, cut] = flat[0:CLASSES]
        g2n[:, cut] = flat[NBR_AT:NBR_AT + CLASSES]
        store(g2s.at[:, cut], outs[4].at[:, cut])
        store(g2n.at[:, cut], outs[5].at[:, cut])
    for copied in stores:
        copied.wait()


def per_device(
    features, self_ids, nbr_ids, nbr_counts, w1_self, w1_nbr, bias1, w2_self, w2_nbr, bias2, labels, top_ids, top_counts
):
    hidden = bias1.shape[0]
    operands = (
        features.T, self_ids.T, jnp.transpose(nbr_ids, (2, 1, 0)), nbr_counts.T, w1_self, w1_nbr,
        bias1.reshape(NG, SPAN), w2_self.T, w2_nbr.T, bias2.reshape(1, CLASSES), labels.reshape(1, 8),
        top_ids, top_counts.reshape(1, 8),
    )
    scratch = [VMEM(a.shape, a.dtype) for a in operands] + [
        VMEM((LOW // SPAN, HIGH * 8, SPAN), f32),
        VMEM((HIGH * COLS, LOW), bf16),
        VMEM((16, hidden), f32),
        VMEM((NG, 16, SPAN), bf16),
        VMEM((NG, 16, SPAN), bf16),
        VMEM((4, 4, SPAN, SPAN), bf16),
        VMEM((NG, 8, SPAN), f32),
        VMEM((8, SPAN, SPAN), f32),
        VMEM((8 * SPAN, SPAN), f32),
        VMEM((8, 16, SPAN), bf16),
        VMEM((NZ, 16, SPAN), bf16),
        VMEM((NZ, 16, SPAN), bf16),
        VMEM((2, 4, 16, SPAN), bf16),
        VMEM((NG, 2, 4, 16, SPAN), bf16),
        VMEM((NG, 8, 16, SPAN), bf16),
        VMEM((NG, 8, 2 * SPAN), f32),
        VMEM((NG, 8, 2 * SPAN), f32),
        VMEM((8, 2 * SPAN), f32),
        VMEM((NG, 8, 2 * SPAN), f32),
        VMEM((4, 4, 64, SPAN), bf16),
        VMEM((GRAD_ROWS, SPAN), f32),
        VMEM((4, NY, BLOCK, SPAN), f32),
        VMEM((4, BLOCK, SPAN), f32),
        VMEM((4, BLOCK, SPAN), f32),
        VMEM((NX, NY, PART, SPAN), bf16),
        VMEM((NG, 16, SPAN), f32),
        VMEM((NG, 16, SPAN), f32),
        VMEM((NY, NG, 16, SPAN), bf16),
        pltpu.SemaphoreType.DMA((total_sems,)),
        pltpu.SemaphoreType.DMA((total_sems,)),
        pltpu.SemaphoreType.DMA((len(operands),)),
        pltpu.SemaphoreType.DMA((NP,)),
    ]
    full, g1 = pl.pallas_call(
        step_kernel,
        out_shape=[
            jax.ShapeDtypeStruct((2, NX, NY, PART, SPAN), bf16), jax.ShapeDtypeStruct((NG, 16, SPAN), f32),
        ],
        in_specs=[pl.BlockSpec(memory_space=pltpu.HBM)] * len(operands),
        out_specs=[pl.BlockSpec(memory_space=pltpu.HBM), pl.BlockSpec(memory_space=VMEM)],
        scratch_shapes=scratch,
        compiler_params=pltpu.CompilerParams(
            collective_id=0, has_side_effects=True, vmem_limit_bytes=60 * 2**20
        ),
        name="step",
    )(*operands)
    shapes = (
        (1, 1), (COLS, hidden), (COLS, hidden), (NG, SPAN), (CLASSES, hidden), (CLASSES, hidden), (1, CLASSES),
    )
    loss, g1s, g1n, gb1, g2s, g2n, gb2 = pl.pallas_call(
        finish_kernel,
        out_shape=[jax.ShapeDtypeStruct(s, f32) for s in shapes],
        in_specs=[pl.BlockSpec(memory_space=pltpu.HBM)] * 2,
        out_specs=[pl.BlockSpec(memory_space=pltpu.HBM)] * len(shapes),
        scratch_shapes=[VMEM(s, f32) for s in shapes] + [
            VMEM(full.shape, bf16), VMEM(g1.shape, f32),
            pltpu.SemaphoreType.DMA((NG + 1,)), pltpu.SemaphoreType.DMA((5 + 2 * NG,)),
        ],
        compiler_params=pltpu.CompilerParams(vmem_limit_bytes=60 * 2**20),
        name="finish",
    )(full, g1)
    return loss.reshape(()), g1s, g1n, gb1.reshape(hidden), g2s.T, g2n.T, gb2.reshape(CLASSES)


def solution(mesh):
    in_specs = (
        P(None, "cols"), P(None, "rep"), P(None, "rep", None), P(None, "rep"), P("cols", None), P("cols", None),
        P(), P(), P(), P(), P(("cols", "rep")), P(("cols", "rep"), None), P(("cols", "rep")),
    )
    out_specs = (P(), P("cols", None), P("cols", None), P(), P(), P(), P())
    return jax.shard_map(per_device, mesh=mesh, in_specs=in_specs, out_specs=out_specs, check_vma=False)
```
